32 devices in a mesh: batch: 4 (over y, x), tm: 8 (over z, core).
Axes of the slice: x: 2, y: 2, z: 4, core: 2. Of those that a mesh axis runs over, the one named last changes fastest.
Arguments:
- clips_in: bfloat16 [16, 128, 32768], P('batch', None, 'tm'), may hold values from -6 to 6
- conv_weight: bfloat16 [64, 64, 4], replicated, may hold values from -0.375 to 0.375
- conv_bias: float32 [64], replicated, may hold values from -3 to 3
- dilated_weight: bfloat16 [64, 64, 3], replicated, may hold values from -0.4375 to 0.4375
- dilated_bias: float32 [64], replicated, may hold values from -3 to 3
- mix_weight: bfloat16 [64, 64], replicated, may hold values from -0.75 to 0.75
- mix_bias: float32 [64], replicated, may hold values from -3 to 3
- frame_counts: int32 [16], P('batch'), may hold values from 16384 to 65536, as said below
- rate_groups: int32 [16], P('batch'), may hold values from 0 to 1
- out_grad: bfloat16 [16, 64, 32768], P('batch', None, 'tm'), may hold values from -6 to 6
Outputs:
- layer_out: bfloat16 [16, 64, 32768], P('batch', None, 'tm')
- clips_grad: bfloat16 [16, 128, 32768], P('batch', None, 'tm')
- conv_weight_grad: float32 [64, 64, 4], replicated
- conv_bias_grad: float32 [64], replicated
- dilated_weight_grad: float32 [64, 64, 3], replicated
- dilated_bias_grad: float32 [64], replicated
- mix_weight_grad: float32 [64, 64], replicated
- mix_bias_grad: float32 [64], replicated
The draws below stay inside these ranges and needn't reach their ends.
Inputs may be any that keep to these rules, and one draw needn't show every extreme that they name: `frame_counts`: in each aligned block of 4 clips one clip, chosen by the seed, has count 2 * 32768 and group 0 in even blocks, 1 in odd blocks.
All inputs are finite; a program needn't handle non-finite values.
Results may differ from the reference program's by a relative error of at most 0.0065.
Values may be sent and summed in bfloat16 or wider, within the bound.
A program may use at most 64 MiB of HBM per device.

```python
import jax
import jax.numpy as jnp
from jax import lax

C = 64
KERNEL = 4
DILATION = 27
CLIPS_DEV = 4
FRAMES = 32768
CLIPS = 16


def clip_table(key):
    key_count, key_group, key_pick = jax.random.split(key, 3)
    counts = jax.random.randint(key_count, (CLIPS,), FRAMES // 2, 2 * FRAMES + 1)
    groups = jax.random.randint(key_group, (CLIPS,), 0, 2)
    picked = jax.random.randint(key_pick, (CLIPS // CLIPS_DEV,), 0, CLIPS_DEV)
    order = jnp.arange(CLIPS)
    block_index = order // CLIPS_DEV
    full = order % CLIPS_DEV == picked[block_index]
    counts = jnp.where(full, 2 * FRAMES, counts)
    groups = jnp.where(full, block_index % 2, groups)
    return (counts.astype(jnp.int32), groups.astype(jnp.int32))


def draw_frame_counts(key, part):
    return clip_table(key)[0]


def draw_rate_groups(key, part):
    return clip_table(key)[1]


def block_levels(own_key, dims, cuts, smallest, high):
    factor_of = 1.0
    for dim, blocks in cuts:
        draws = jax.random.uniform(jax.random.fold_in(jax.random.fold_in(own_key, 6), dim), (blocks,), jnp.float32, smallest / len(cuts), high / len(cuts))
        factor_of = factor_of * jnp.repeat(jnp.exp(draws), dims[dim] // blocks).reshape((-1,) + (1,) * (len(dims) - 1 - dim))
    return factor_of


def gaussian(stream_key, dims, scale, limit, pieces=(), kind=jnp.bfloat16):
    array = scale * jax.random.normal(stream_key, dims, jnp.float32)
    if pieces:
        array = array * block_levels(stream_key, dims, pieces, -0.22, 0.18)
    return jnp.clip(array, -limit, limit).astype(kind)


def setup_inputs(seed: int = 0) -> dict:
    streams_of = jax.random.split(jax.random.key(seed), 11)
    return {
        "clips_in": gaussian(streams_of[0], (CLIPS, 2 * C, FRAMES), 1.0, 6.0, ((0, 4), (2, 8))),
        "conv_weight": gaussian(streams_of[1], (C, C, KERNEL), (C * KERNEL) ** -0.5, 0.375),
        "conv_bias": gaussian(streams_of[2], (C,), 0.5, 3.0, (), jnp.float32),
        "dilated_weight": gaussian(streams_of[3], (C, C, 3), (C * 3) ** -0.5, 0.4375),
        "dilated_bias": gaussian(streams_of[4], (C,), 0.5, 3.0, (), jnp.float32),
        "mix_weight": gaussian(streams_of[5], (C, C), C ** -0.5, 0.75),
        "mix_bias": gaussian(streams_of[6], (C,), 0.5, 3.0, (), jnp.float32),
        "frame_counts": draw_frame_counts(jax.random.fold_in(streams_of[10], 71), 0),
        "rate_groups": draw_rate_groups(jax.random.fold_in(streams_of[10], 71), 0),
        "out_grad": gaussian(streams_of[9], (CLIPS, C, FRAMES), 1.0, 6.0, ((0, 4), (2, 8))),
    }


@jax.custom_vjp
def low(v):
    return lax.optimization_barrier(v.astype(jnp.bfloat16)).astype(jnp.float32)

@jax.custom_vjp
def low_back(v):
    return v

def low_keep(v):
    return (low(v), None)

def low_pass(kept, grad):
    return (grad,)

def back_keep(v):
    return (v, None)

def back_low(kept, grad):
    return (low(grad),)
low.defvjp(low_keep, low_pass)
low_back.defvjp(back_keep, back_low)

def convolve(signal, kernel, stride, margin, spread):
    return lax.conv_general_dilated(signal[None], kernel, window_strides=(stride,), padding=[(margin, margin)], rhs_dilation=(spread,), dimension_numbers=('NCH', 'OIH', 'NCH'), precision=lax.Precision.HIGHEST)[0]

def forward(clip, conv_w, conv_b, dilated_w, dilated_b, mix_w, mix_b, valid_len):
    channels = conv_w.shape[0]
    frames_in = clip.reshape(2, channels, FRAMES).transpose(1, 2, 0).reshape(channels, 2 * FRAMES)
    out_mask = (jnp.arange(FRAMES, dtype=jnp.int32) < valid_len).astype(jnp.float32)
    in_mask = (jnp.arange(2 * FRAMES, dtype=jnp.int32) < 2 * valid_len).astype(jnp.float32)
    masked = frames_in * in_mask[None, :]
    first_out = low_back((convolve(masked, conv_w, 2, 1, 1) + conv_b[:, None]) * out_mask[None, :])
    mid_act = low(jax.nn.gelu(first_out))
    dilated_pre = low_back(convolve(mid_act, dilated_w, 1, DILATION, DILATION) + dilated_b[:, None])
    gated = low(jax.nn.gelu(dilated_pre))
    branch = jnp.dot(mix_w, gated, precision=lax.Precision.HIGHEST) + mix_b[:, None]
    return (first_out + branch) * out_mask[None, :]

def reference(clips_in, conv_weight, conv_bias, dilated_weight, dilated_bias, mix_weight, mix_bias, frame_counts, rate_groups, out_grad):
    valid = jnp.minimum(frame_counts // (1 + rate_groups), FRAMES).astype(jnp.int32)
    params = tuple((p.astype(jnp.float32) for p in (conv_weight, conv_bias, dilated_weight, dilated_bias, mix_weight, mix_bias)))

    def one_clip(totals, items):
        clip, cotangent, valid_len = items

        def apply(clip_f, *weights):
            return forward(clip_f, *weights, valid_len)
        result, pull = jax.vjp(apply, clip.astype(jnp.float32), *params)
        grads = pull(cotangent.astype(jnp.float32))
        totals = tuple((t + g for t, g in zip(totals, grads[1:])))
        return (totals, (result.astype(jnp.bfloat16), grads[0].astype(jnp.bfloat16)))
    start = tuple((jnp.zeros(p.shape, jnp.float32) for p in params))
    totals, (layer_out, clips_grad) = lax.scan(one_clip, start, (clips_in, out_grad, valid))
    return (layer_out, clips_grad, totals[0], totals[1], totals[2], totals[3], totals[4], totals[5])
```

```python
import functools

import jax
import jax.numpy as jnp
from jax import lax
from jax.experimental import pallas as pl
from jax.experimental.pallas import tpu as pltpu
from jax.sharding import PartitionSpec as P

DILATION = 27
EDGE = 128
CHUNK = 2048
PIECE = 32
MESH = pl.DeviceIdType.MESH
F32 = jnp.float32
BF16 = jnp.bfloat16
C0 = 0.7978845608028654
C1 = 0.044715


def dot(a, b):
    return lax.dot_general(a, b, (((1,), (0,)), ((), ())), preferred_element_type=F32)


def dot_t(a, b):
    return lax.dot_general(a, b, (((1,), (1,)), ((), ())), preferred_element_type=F32)


def gelu_parts(x):
    square = x * x
    s = 0.5 + 0.5 * jnp.tanh(x * (C0 + (C0 * C1) * square))
    value = x * s
    slope = s + (value - value * s) * (2 * C0 + (6 * C0 * C1) * square)
    return value, slope


def tall(rows, copies):
    return jnp.concatenate([rows] * copies, axis=0)


def wide(tile, count):
    return jnp.concatenate([tile] * count, axis=1)


def lane_groups(value):
    total = value[:, :EDGE]
    for start in range(EDGE, value.shape[1], EDGE):
        total = total + value[:, start : start + EDGE]
    return total


def compute(
    span,
    total,
    chunk,
    place,
    counts,
    groups,
    x_ref,
    xh_ref,
    og_ref,
    ogh_ref,
    wc,
    wd,
    wm,
    wdt,
    wct,
    biases,
    out_ref,
    clips_ref,
    sums_ref,
    pconv,
    pdil,
    pmix,
    psum,
    xs,
    bg,
    first,
    slope1,
    mid,
    midm,
    midp,
    x1m,
    x0p,
    pre,
    prem,
    prep,
    grad,
    gradm,
    gradp,
):
    ch = 64
    b = pl.program_id(0)
    off = 2 * EDGE
    base = place[0] * span
    valid = jnp.minimum(lax.shift_right_logical(counts[b], groups[b]), total)

    @pl.when(b == 0)
    def _():
        for ref in (xs, mid, midm, midp, x1m, x0p, pre, prem, prep, grad, gradm, gradp):
            for start in (0, span + 3 * EDGE):
                ref[:, start : start + EDGE] = jnp.zeros((ref.shape[0], EDGE), ref.dtype)
        for ref in (pconv, pdil, pmix, psum):
            ref[...] = jnp.zeros(ref.shape, ref.dtype)

    def mask_rows(t, n):
        frame = base + t + lax.broadcasted_iota(jnp.int32, (16, n), 1)
        return ((frame >= 0) & (frame < valid)).astype(F32)

    def put(ref, start, value):
        ref[:, start : start + value.shape[1]] = value

    def stage0(t, n):
        low = tall(mask_rows(t, n).astype(BF16), ch // 16)
        if t < 0:
            x, og = xh_ref[0, 0], ogh_ref[0, 0]
        elif t >= span:
            x, og = xh_ref[0, 1], ogh_ref[0, 1]
        else:
            x, og = x_ref[0, :, t : t + n], og_ref[0, :, t : t + n]
        dst = slice(t + off, t + off + n)
        even = x[:ch] * low
        odd = x[ch:] * low
        xs[:ch, dst] = even
        xs[ch:, dst] = odd
        put(x1m, t + off + 1, odd)
        put(x0p, t + off - 1, even)
        bg[:, dst] = og * low

    def stage1(t, n):
        here = slice(t + off, t + off + n)
        taps = jnp.concatenate([x1m[:, here], xs[:, here], x0p[:, here]], axis=0)
        mask = tall(mask_rows(t, n), ch // 16)
        f = (dot(wc[...], taps) + wide(biases[0], n // EDGE)) * mask
        value, slope = gelu_parts(f)
        first[:, here] = f
        slope1[:, here] = slope
        low = value.astype(BF16)
        mid[:, here] = low
        put(midm, t + off + DILATION, low)
        put(midp, t + off - DILATION, low)

    def stage2(t, n):
        here = slice(t + off, t + off + n)
        inner = 0 <= t < span
        taps = jnp.concatenate([midm[:, here], mid[:, here], midp[:, here]], axis=0)
        dilated = dot(wd[...], taps) + wide(biases[1], n // EDGE)
        value, slope = gelu_parts(dilated)
        branch_grad = bg[:, here]
        if inner:
            gated = value.astype(BF16)
            both = dot(wm[...], jnp.concatenate([gated, branch_grad], axis=0))
            mask = tall(mask_rows(t, n), ch // 16)
            layer = (first[:, here] + both[:ch] + wide(biases[2], n // EDGE)) * mask
            out_ref[0, :, t : t + n] = layer.astype(BF16)
            up = both[ch:]
            pmix[...] += dot_t(branch_grad, gated)
            psum[2] += lane_groups(branch_grad.astype(F32))
        else:
            up = dot(wm[ch:, ch:], branch_grad)
        pg = (up * slope).astype(BF16)
        pre[:, here] = pg
        put(prem, t + off + DILATION, pg)
        put(prep, t + off - DILATION, pg)
        if inner:
            psum[1] += lane_groups(pg.astype(F32))

    def stage3(t, n):
        here = slice(t + off, t + off + n)
        before = prem[:, here]
        now = pre[:, here]
        taps = jnp.concatenate([prep[:, here], now, before], axis=0)
        mid_grad = dot(wdt[...], taps)
        mask = tall(mask_rows(t, n), ch // 16)
        g = ((bg[:, here].astype(F32) + mid_grad * slope1[:, here]) * mask).astype(BF16)
        grad[:, here] = g
        put(gradm, t + off + 1, g)
        put(gradp, t + off - 1, g)
        if 0 <= t < span:
            pdil[...] += dot_t(
                jnp.concatenate([now, before], axis=0),
                jnp.concatenate([mid[:, here], midm[:, here]], axis=0),
            )
            psum[0] += lane_groups(g.astype(F32))

    def stage4(t, n):
        here = slice(t + off, t + off + n)
        g = grad[:, here]
        before = gradm[:, here]
        y = jnp.concatenate([x1m[:, here], xs[:ch, here]], axis=0)
        if t < span:
            after = gradp[:, here]
            low = tall(mask_rows(t, n), 2 * ch // 16)
            dx = dot(wct[...], jnp.concatenate([before, g, after], axis=0)) * low
            clips_ref[0, :, t : t + n] = dx.astype(BF16)
        if t == 0:
            lane = lax.broadcasted_iota(jnp.int32, (16, n), 1)
            own = tall((lane > 0).astype(F32).astype(BF16), ch // 16)
            before = before * own
        pconv[...] += dot_t(jnp.concatenate([g, before], axis=0), y)

    def stage4_edge():
        t, n = span, EDGE
        here = slice(t + off, t + off + n)
        before = gradm[:, here]
        lane = lax.broadcasted_iota(jnp.int32, (16, n), 1)
        own = tall((lane == 0).astype(F32).astype(BF16), ch // 16)
        y = jnp.concatenate([x1m[:, here], xs[:ch, here]], axis=0)
        pconv[ch:, :] += dot_t(before * own, y)

    inner = [(t, chunk) for t in range(0, span, chunk)]
    pieces = [(-EDGE, EDGE)] + inner + [(span, EDGE)]
    count = len(pieces)
    for step in range(count + 6):
        if 0 <= step - 6 < count and 0 <= pieces[step - 6][0] < span:
            stage4(*pieces[step - 6])
        if 0 <= step - 4 < count:
            stage3(*pieces[step - 4])
        if 0 <= step - 2 < count:
            stage2(*pieces[step - 2])
        if step == 0:
            stage0(*pieces[0])
        if step + 1 < count:
            stage0(*pieces[step + 1])
        if step < count:
            stage1(*pieces[step])
    stage4_edge()

    @pl.when(b == pl.num_programs(0) - 1)
    def _():
        rows = [pconv[...], pdil[:ch, :], jnp.concatenate([pdil[ch:, :ch], pmix[...]], axis=1)]
        at = 0
        for block in rows:
            sums_ref[at : at + block.shape[0], :] = block.astype(BF16)
            at += block.shape[0]
        lines = [jnp.sum(psum[k].T, axis=0, keepdims=True) for k in range(3)]
        lines = jnp.concatenate(lines + [jnp.zeros((13, ch), F32)], axis=0)
        lines = jnp.concatenate([lines, jnp.zeros_like(lines)], axis=1)
        sums_ref[at : at + 16, :] = lines.astype(BF16)
        sums_ref[at + 16 :, :] = jnp.zeros((sums_ref.shape[0] - at - 16, 2 * ch), BF16)


def compute_call(span, total, clips, chunk, rows=288):
    ch = 64
    lanes = span + 4 * EDGE
    whole = lambda shape: pl.BlockSpec(shape, lambda b: (0,) * len(shape))
    smem = pl.BlockSpec(memory_space=pltpu.SMEM)
    clip = lambda *shape: pl.BlockSpec((1, *shape), lambda b: (b,) + (0,) * len(shape))
    sums = [(2 * ch, 2 * ch), (2 * ch, 2 * ch), (ch, ch), (3, ch, EDGE)]
    return pl.pallas_call(
        functools.partial(compute, span, total, chunk),
        name="layer",
        grid=(clips,),
        in_specs=[smem, smem, smem, clip(2 * ch, span), clip(2, 2 * ch, EDGE), clip(ch, span), clip(2, ch, EDGE)]
        + [whole(s) for s in ((ch, 4 * ch), (ch, 3 * ch), (2 * ch, 2 * ch), (ch, 3 * ch), (2 * ch, 3 * ch), (3, ch, EDGE))],
        out_specs=[clip(ch, span), clip(2 * ch, span), whole((rows, 2 * ch))],
        out_shape=[
            jax.ShapeDtypeStruct((clips, ch, span), BF16),
            jax.ShapeDtypeStruct((clips, 2 * ch, span), BF16),
            jax.ShapeDtypeStruct((rows, 2 * ch), BF16),
        ],
        scratch_shapes=[pltpu.VMEM(s, F32) for s in sums]
        + [pltpu.VMEM((2 * ch, lanes), BF16)]
        + [pltpu.VMEM((ch, lanes), BF16)]
        + [pltpu.VMEM((ch, lanes), F32)] * 2
        + [pltpu.VMEM((ch, lanes), BF16)] * 11,
        compiler_params=pltpu.CompilerParams(vmem_limit_bytes=63 << 20),
    )


def edges(
    parts,
    x_ref,
    og_ref,
    cw,
    dw,
    mw,
    cb,
    db,
    mb,
    xh_ref,
    ogh_ref,
    wc,
    wd,
    wm,
    wdt,
    wct,
    biases,
    xzero,
    ogzero,
    send,
    recv,
    fill,
):
    ch = 64
    span = x_ref.shape[2]
    row, place = lax.axis_index("batch"), lax.axis_index("tm")
    has = (place > 0, place < parts - 1)
    other = (place - 1, place + 1)
    barrier = pltpu.get_barrier_semaphore()
    for side in range(2):
        @pl.when(has[side])
        def _():
            pl.semaphore_signal(barrier, inc=1, device_id=(row, other[side]), device_id_type=MESH)
    xzero[...] = jnp.zeros(xzero.shape, BF16)
    ogzero[...] = jnp.zeros(ogzero.shape, BF16)
    peers = jnp.where(has[0], 1, 0) + jnp.where(has[1], 1, 0)
    pl.semaphore_wait(barrier, peers)

    def moves(side):
        cut = pl.ds(0, EDGE) if side == 0 else pl.ds(span - EDGE, EDGE)
        return [
            pltpu.make_async_remote_copy(
                src_ref=src.at[:, :, cut],
                dst_ref=dst.at[:, 1 - side],
                send_sem=send.at[side, k],
                recv_sem=recv.at[1 - side, k],
                device_id=(row, other[side]),
                device_id_type=MESH,
            )
            for k, (src, dst) in enumerate(((x_ref, xh_ref), (og_ref, ogh_ref)))
        ]

    def blanks(side):
        return [
            pltpu.make_async_copy(zero, dst.at[:, side], fill.at[side, k])
            for k, (zero, dst) in enumerate(((xzero, xh_ref), (ogzero, ogh_ref)))
        ]

    for side in range(2):
        @pl.when(has[side])
        def _():
            for move in moves(side):
                move.start()

        @pl.when(jnp.logical_not(has[side]))
        def _():
            for blank in blanks(side):
                blank.start()

    taps = [cw[:, k, :] for k in range(4)]
    flip = lambda w: w.astype(F32).T.astype(BF16)
    zero = jnp.zeros((ch, ch), BF16)
    for k in range(4):
        wc[:, k * ch : (k + 1) * ch] = taps[k]
    for k in range(3):
        wd[:, k * ch : (k + 1) * ch] = dw[k]
        wdt[:, k * ch : (k + 1) * ch] = flip(dw[k])
    wm[...] = jnp.concatenate(
        [jnp.concatenate([mw[...], zero], axis=1), jnp.concatenate([zero, flip(mw[...])], axis=1)], axis=0
    )
    back = [flip(tap) for tap in taps]
    wct[:ch, :] = jnp.concatenate([back[3], back[1], zero], axis=1)
    wct[ch:, :] = jnp.concatenate([zero, back[2], back[0]], axis=1)
    for k, line in enumerate((cb, db, mb)):
        biases[k] = jnp.broadcast_to(line[...], (EDGE, ch)).T

    for side in range(2):
        @pl.when(has[side])
        def _():
            for move in moves(side):
                move.wait_send()
            for move in moves(1 - side):
                move.wait_recv()

        @pl.when(jnp.logical_not(has[side]))
        def _():
            for blank in blanks(side):
                blank.wait()


def edges_call(clips, span, parts):
    ch = 64
    vmem = pl.BlockSpec(memory_space=pltpu.VMEM)
    hbm = pl.BlockSpec(memory_space=pl.ANY)
    shapes = [(ch, 4 * ch), (ch, 3 * ch), (2 * ch, 2 * ch), (ch, 3 * ch), (2 * ch, 3 * ch)]
    return pl.pallas_call(
        functools.partial(edges, parts),
        name="edges",
        in_specs=[hbm, hbm] + [vmem] * 6,
        out_specs=[hbm, hbm] + [vmem] * 6,
        out_shape=[
            jax.ShapeDtypeStruct((clips, 2, 2 * ch, EDGE), BF16),
            jax.ShapeDtypeStruct((clips, 2, ch, EDGE), BF16),
        ]
        + [jax.ShapeDtypeStruct(s, BF16) for s in shapes]
        + [jax.ShapeDtypeStruct((3, ch, EDGE), F32)],
        scratch_shapes=[
            pltpu.VMEM((clips, 2 * ch, EDGE), BF16),
            pltpu.VMEM((clips, ch, EDGE), BF16),
            pltpu.SemaphoreType.DMA((2, 2)),
            pltpu.SemaphoreType.DMA((2, 2)),
            pltpu.SemaphoreType.DMA((2, 2)),
        ],
        compiler_params=pltpu.CompilerParams(collective_id=0, has_side_effects=True, vmem_limit_bytes=63 << 20),
    )


def owner_list(rows, parts, pieces):
    half = parts // 2
    order = sorted(range(half), key=lambda q: abs(2 * q - half + 1))
    spots = [(r, 2 * q + 1) for q in order for r in range(rows)]
    spots += [(r, 2 * q) for q in order for r in range(rows)]
    return spots[:pieces]


def total_kernel(rows, parts, owners, x, out, slots, send, recv, send2, recv2):
    count = rows * parts
    pieces = len(owners)
    row, place = lax.axis_index("batch"), lax.axis_index("tm")
    me = row * parts + place
    barrier = pltpu.get_barrier_semaphore()

    def others(action):
        def step(r, carry):
            target = lax.rem(me + r, count)
            action(target // parts, lax.rem(target, parts))
            return carry

        lax.fori_loop(1, count, step, 0)

    others(lambda r, p: pl.semaphore_signal(barrier, inc=1, device_id=(r, p), device_id_type=MESH))
    pl.semaphore_wait(barrier, count - 1)
    for piece, (r, p) in enumerate(owners):
        home = r * parts + p

        @pl.when(me != home)
        def _():
            pltpu.make_async_remote_copy(
                src_ref=x.at[piece],
                dst_ref=slots.at[lax.rem(me - home + count, count) - 1],
                send_sem=send,
                recv_sem=recv,
                device_id=(r, p),
                device_id_type=MESH,
            ).start()

    for piece, (r, p) in enumerate(owners):
        @pl.when(me == r * parts + p)
        def _():
            pltpu.make_async_copy(slots, slots, recv).wait()
            total = x[piece].astype(F32)
            for k in range(count - 1):
                total = total + slots[k].astype(F32)
            out[piece] = total.astype(BF16)
            others(
                lambda tr, tp: pltpu.make_async_remote_copy(
                    src_ref=out.at[piece],
                    dst_ref=out.at[piece],
                    send_sem=send2,
                    recv_sem=recv2,
                    device_id=(tr, tp),
                    device_id_type=MESH,
                ).start()
            )

    owner = functools.reduce(jnp.logical_or, [me == r * parts + p for r, p in owners])

    @pl.when(owner)
    def _():
        rest = out.at[pl.ds(0, pieces - 1)]
        pltpu.make_async_copy(rest, rest, recv2).wait()
        sent = x.at[pl.ds(0, pieces - 1)]
        pltpu.make_async_copy(sent, sent, send).wait()
        pltpu.make_async_copy(slots, slots, send2).wait()

    @pl.when(jnp.logical_not(owner))
    def _():
        pltpu.make_async_copy(out, out, recv2).wait()
        pltpu.make_async_copy(x, x, send).wait()


def total_call(rows, parts, pieces):
    shape = (pieces, PIECE, 128)
    vmem = pl.BlockSpec(memory_space=pltpu.VMEM)
    return pl.pallas_call(
        functools.partial(total_kernel, rows, parts, owner_list(rows, parts, pieces)),
        name="total",
        in_specs=[vmem],
        out_specs=vmem,
        out_shape=jax.ShapeDtypeStruct(shape, BF16),
        scratch_shapes=[pltpu.VMEM((rows * parts - 1, PIECE, 128), BF16)] + [pltpu.SemaphoreType.DMA] * 4,
        compiler_params=pltpu.CompilerParams(collective_id=1, has_side_effects=True, vmem_limit_bytes=63 << 20),
    )


def unpack(sums, cg, cb, dg, db, mg, mb):
    ch = 64
    at = lambda start, count: sums[start : start + count, :].astype(F32)
    low, high = at(0, ch), at(ch, ch)
    for k, block in enumerate((low[:, :ch], low[:, ch:], high[:, :ch], high[:, ch:])):
        cg[:, k, :] = block
    block = at(2 * ch, ch)
    dg[1] = block[:, :ch]
    dg[0] = block[:, ch:]
    block = at(3 * ch, ch)
    dg[2] = block[:, :ch]
    mg[...] = block[:, ch:]
    lines = at(4 * ch, 16)[:, :ch]
    for k, ref in enumerate((cb, db, mb)):
        ref[...] = lines[k : k + 1]


def unpack_call():
    ch = 64
    vmem = pl.BlockSpec(memory_space=pltpu.VMEM)
    shapes = [(ch, 4, ch), (1, ch), (3, ch, ch), (1, ch), (ch, ch), (1, ch)]
    return pl.pallas_call(
        unpack,
        name="unpack",
        in_specs=[vmem],
        out_specs=[vmem] * 6,
        out_shape=[jax.ShapeDtypeStruct(s, F32) for s in shapes],
    )


def body(rows, parts, clips_in, cw, cb, dw, db, mw, mb, counts, groups, out_grad):
    clips, ch, span = out_grad.shape
    pieces = -(-(4 * ch + 16) // PIECE)
    place = lax.axis_index("tm").astype(jnp.int32)[None]
    xh, ogh, *params = edges_call(clips, span, parts)(
        clips_in, out_grad, cw.transpose(0, 2, 1), dw.transpose(2, 0, 1), mw, cb[None], db[None], mb[None]
    )
    layer_out, clips_grad, sums = compute_call(span, span * parts, clips, CHUNK, pieces * PIECE)(
        place, counts, groups, clips_in, xh, out_grad, ogh, *params
    )
    sums = total_call(rows, parts, pieces)(sums.reshape(pieces, PIECE, 2 * ch))
    cg, cbg, dg, dbg, mg, mbg = unpack_call()(sums.reshape(pieces * PIECE, 2 * ch))
    return (layer_out, clips_grad, cg.transpose(0, 2, 1), cbg[0], dg.transpose(1, 2, 0), dbg[0], mg, mbg[0])


def solution(mesh):
    split = P("batch", None, "tm")
    placed = (split, P(), P(), P(), P(), P(), P(), P("batch"), P("batch"), split)
    return jax.shard_map(
        functools.partial(body, mesh.shape["batch"], mesh.shape["tm"]),
        mesh=mesh,
        in_specs=placed,
        out_specs=(split, split) + (P(),) * 6,
        check_vma=False,
    )
```

```python
import functools

import jax
import jax.numpy as jnp
from jax import lax
from jax.experimental import pallas as pl
from jax.experimental.pallas import tpu as pltpu
from jax.sharding import PartitionSpec as P

DILATION = 27
EDGE = 128
OFF = 2 * EDGE
CHUNK = 2048
PIECE = 32
MESH = pl.DeviceIdType.MESH
F32 = jnp.float32
BF16 = jnp.bfloat16
C0 = 0.7978845608028654
C1 = 0.044715


def dot(a, b):
    return lax.dot_general(a, b, (((1,), (0,)), ((), ())), preferred_element_type=F32)


def dot_t(a, b):
    return lax.dot_general(a, b, (((1,), (1,)), ((), ())), preferred_element_type=F32)


def stack(*rows):
    return jnp.concatenate(rows, axis=0)


def beside(*parts):
    return jnp.concatenate(parts, axis=1)


def gelu_parts(half):
    square = half * half
    t = jnp.tanh(half * (2 * C0 + (8 * C0 * C1) * square))
    up = 1.0 + t
    value = half * up
    return value, up + (value * (1.0 - t)) * (2 * C0 + (24 * C0 * C1) * square)


def tall(rows, copies):
    return jnp.concatenate([rows] * copies, axis=0)


def wide(tile, count):
    return jnp.concatenate([tile] * count, axis=1)


def lane_groups(value):
    total = value[:, :EDGE]
    for start in range(EDGE, value.shape[1], EDGE):
        total = total + value[:, start : start + EDGE]
    return total


def owner_list(rows, parts, pieces):
    half = parts // 2
    order = sorted(range(half), key=lambda q: abs(2 * q - half + 1))
    spots = [(r, 2 * q + 1) for q in order for r in range(rows)]
    spots += [(r, 2 * q) for q in order for r in range(rows)]
    return spots[:pieces]


def layer(
    rows,
    parts,
    owners,
    counts,
    groups,
    x_ref,
    og_ref,
    cw,
    dw,
    mw,
    cb,
    db,
    mb,
    outs,
    dxs,
    total_ref,
    wc,
    wd,
    wm,
    wu,
    wdt,
    wct,
    biases,
    x0,
    x1,
    bg,
    x0p,
    x1m,
    half,
    slope,
    mid,
    midm,
    midp,
    gated,
    pre,
    prem,
    prep,
    grad,
    gradm,
    gradp,
    xh,
    ogh,
    pconv,
    pdil,
    pmix,
    psum,
    parcel,
    slots,
    in_sem,
    send,
    recv,
    send1,
    recv1,
    send2,
    recv2,
):
    ch = 64
    clips, _, span = og_ref.shape
    chunk = min(CHUNK, span)
    pieces = len(owners)
    count = rows * parts
    row, place = lax.axis_index("batch"), lax.axis_index("tm")
    me = row * parts + place
    base = place * span

    def others(action):
        def step(r, carry):
            target = lax.rem(me + r, count)
            action(target // parts, lax.rem(target, parts))
            return carry

        lax.fori_loop(1, count, step, 0)

    inside = pl.ds(OFF, span)

    def fetches(b):
        return [
            pltpu.make_async_copy(x_ref.at[b, pl.ds(0, ch)], x0.at[b, :, inside], in_sem.at[b, 0]),
            pltpu.make_async_copy(x_ref.at[b, pl.ds(ch, ch)], x1.at[b, :, inside], in_sem.at[b, 1]),
            pltpu.make_async_copy(og_ref.at[b], bg.at[b, :, inside], in_sem.at[b, 2]),
        ]

    for b in range(clips):
        for fetch in fetches(b):
            fetch.start()
    xh[...] = jnp.zeros(xh.shape, BF16)
    ogh[...] = jnp.zeros(ogh.shape, BF16)
    barrier = pltpu.get_barrier_semaphore()
    others(lambda r, p: pl.semaphore_signal(barrier, inc=1, device_id=(r, p), device_id_type=MESH))

    flip = lambda w: w.astype(F32).T.astype(BF16)
    taps = [cw[:, k, :] for k in range(4)]
    zero = jnp.zeros((ch, ch), BF16)
    for k in range(4):
        wc[:, k * ch : (k + 1) * ch] = taps[k] * 0.5
    for k in range(3):
        wd[:, k * ch : (k + 1) * ch] = dw[k] * 0.5
        wdt[:, k * ch : (k + 1) * ch] = flip(dw[k]) * 0.5
    wm[...] = mw[...] * 0.5
    wu[...] = flip(mw[...]) * 0.5
    back = [flip(tap) for tap in taps]
    wct[:ch, :] = beside(back[3], back[1], zero)
    wct[ch:, :] = beside(zero, back[2], back[0])
    for k, line in enumerate((cb, db, mb)):
        biases[k] = jnp.broadcast_to(line[...] * 0.5, (EDGE, ch)).T

    left, right = pl.ds(OFF - EDGE, EDGE), pl.ds(OFF + span, EDGE)
    for ref in (gradm,):
        ref[:, :, OFF : OFF + EDGE] = jnp.zeros((clips, ch, EDGE), BF16)
    for ref in (x0, x1, mid, grad, gradm):
        ref[:, :, 0:EDGE] = jnp.zeros((clips, ch, EDGE), BF16)
        ref[:, :, OFF + span : OFF + span + EDGE] = jnp.zeros((clips, ch, EDGE), BF16)
        ref[:, :, OFF + span + EDGE :] = jnp.zeros((clips, ch, EDGE), BF16)
    for ref in (x0p, x1m, midm, midp, prem, prep):
        for at in (0, OFF + span, OFF + span + EDGE):
            ref[:, :, at : at + EDGE] = jnp.zeros((clips, ch, EDGE), BF16)
    for ref in (pconv, pdil, pmix, psum):
        ref[...] = jnp.zeros(ref.shape, F32)

    def masks(b, t, n, high=1.0):
        valid = jnp.minimum(lax.shift_right_logical(counts[b], groups[b]), span * parts)
        frame = base + t + lax.broadcasted_iota(jnp.int32, (16, n), 1)
        return jnp.where((frame >= 0) & (frame < valid), high, 0.0)

    def put(ref, b, start, value):
        ref[b, :, start : start + value.shape[1]] = value

    has = (place > 0, place < parts - 1)
    other = (place - 1, place + 1)

    def moves(side):
        cut = pl.ds(0, EDGE) if side == 0 else pl.ds(span - EDGE, EDGE)
        return [
            pltpu.make_async_remote_copy(
                src_ref=src.at[:, :, cut],
                dst_ref=dst.at[1 - side],
                send_sem=send.at[side, k],
                recv_sem=recv.at[1 - side, k],
                device_id=(row, other[side]),
                device_id_type=MESH,
            )
            for k, (src, dst) in enumerate(((x_ref, xh), (og_ref, ogh)))
        ]

    def stage1(b, t, n):
        here = slice(t + OFF, t + OFF + n)
        taps = stack(x1m[b, :, here], x0[b, :, here], x1[b, :, here], x0p[b, :, here])
        h = dot(wc[...], taps) + wide(biases[0], n // EDGE)
        value, s = gelu_parts(h)
        half[b, :, here] = h
        slope[b, :, here] = s
        return value

    def shifted(refs, b, t, step, low):
        now, before, after = refs
        now[b, :, t + OFF : t + OFF + low.shape[1]] = low
        put(before, b, t + OFF + step, low)
        put(after, b, t + OFF - step, low)

    def first(b, carry):
        for fetch in fetches(b):
            fetch.wait()
        for t in range(0, span, chunk):
            here = slice(t + OFF, t + OFF + chunk)
            low = tall(masks(b, t, chunk).astype(BF16), ch // 16)
            even = x0[b, :, here] * low
            x0[b, :, here] = even
            put(x0p, b, t + OFF - 1, even)
            put(x1m, b, t + OFF + 1, x1[b, :, here])
            bg[b, :, here] = bg[b, :, here] * low
        for t in range(0, span, chunk):
            start, n = max(t, EDGE), min(t + chunk, span - EDGE) - max(t, EDGE)
            low = tall(masks(b, start, n).astype(BF16), ch // 16)
            shifted((mid, midm, midp), b, start, DILATION, stage1(b, start, n).astype(BF16) * low)

        @pl.when(b == 0)
        def _():
            pl.semaphore_wait(barrier, count - 1)
            for side in range(2):
                @pl.when(has[side])
                def _():
                    for move in moves(side):
                        move.start()

        return carry

    lax.fori_loop(0, clips, first, 0)

    for side in range(2):
        @pl.when(has[side])
        def _():
            for move in moves(1 - side):
                move.wait_recv()

    sides = ((0, -EDGE), (1, span))

    def outside(b, carry):
        lows = [tall(masks(b, t, EDGE).astype(BF16), ch // 16) for _, t in sides]
        for (side, t), low in zip(sides, lows):
            here = slice(t + OFF, t + OFF + EDGE)
            even = xh[side, b, :ch] * low
            odd = xh[side, b, ch:]
            x0[b, :, here] = even
            x1[b, :, here] = odd
            put(x0p, b, t + OFF - 1, even)
            put(x1m, b, t + OFF + 1, odd)
            bg[b, :, here] = ogh[side, b] * low
        starts = (-EDGE, span - EDGE)
        spots = [slice(t + OFF, t + OFF + 2 * EDGE) for t in starts]
        both = lambda ref: beside(*[ref[b, :, spot] for spot in spots])
        h = dot(wc[...], stack(both(x1m), both(x0), both(x1), both(x0p))) + wide(biases[0], 4)
        value, s = gelu_parts(h)
        for k, t in enumerate(starts):
            cut = slice(2 * k * EDGE, 2 * (k + 1) * EDGE)
            half[b, :, spots[k]] = h[:, cut]
            slope[b, :, spots[k]] = s[:, cut]
            low = tall(masks(b, t, 2 * EDGE).astype(BF16), ch // 16)
            shifted((mid, midm, midp), b, t, DILATION, value[:, cut].astype(BF16) * low)
        spots = [slice(t + OFF, t + OFF + EDGE) for _, t in sides]
        d = dot(wd[...], stack(both(midm), both(mid), both(midp))) + wide(biases[1], 2)
        _, s = gelu_parts(d)
        low = (dot(wu[...], both(bg)) * s).astype(BF16)
        for k, (side, t) in enumerate(sides):
            shifted((pre, prem, prep), b, t, DILATION, low[:, k * EDGE : (k + 1) * EDGE])
        return carry

    lax.fori_loop(0, clips, outside, 0)

    ones = jnp.ones((16, chunk), BF16)

    def second(b, carry):
        for t in range(0, span, chunk):
            here = slice(t + OFF, t + OFF + chunk)
            d = dot(wd[...], stack(midm[b, :, here], mid[b, :, here], midp[b, :, here]))
            d = d + wide(biases[1], chunk // EDGE)
            value, s = gelu_parts(d)
            low = value.astype(BF16)
            gated[b, :, t : t + chunk] = low
            pg = dot(wu[...], bg[b, :, here]) * s
            psum[1] += lane_groups(pg)
            shifted((pre, prem, prep), b, t, DILATION, pg.astype(BF16))
            pmix[:, : ch + 16] += dot_t(bg[b, :, here], stack(low, ones))
        for t in range(0, span, chunk):
            here = slice(t + OFF, t + OFF + chunk)
            mask = tall(masks(b, t, chunk), ch // 16)
            mid_grad = dot(wdt[...], stack(prep[b, :, here], pre[b, :, here], prem[b, :, here]))
            g = (bg[b, :, here].astype(F32) + mid_grad * slope[b, :, here]) * mask
            psum[0] += lane_groups(g)
            shifted((grad, gradm, gradp), b, t, 1, g.astype(BF16))
            pdil[...] += dot_t(
                stack(pre[b, :, here], prem[b, :, here]), stack(mid[b, :, here], midm[b, :, here])
            )
        wide_here = slice(OFF, OFF + span + EDGE)
        pconv[...] += dot_t(
            stack(grad[b, :, wide_here], gradm[b, :, wide_here]), stack(x1m[b, :, wide_here], x0[b, :, wide_here])
        )
        return carry

    lax.fori_loop(0, clips, second, 0)

    at = 0
    flat = [
        pconv[...],
        pdil[:ch, :],
        beside(pdil[ch:, :ch], pmix[:, :ch]),
    ]
    lines = [jnp.sum(psum[k].T, axis=0, keepdims=True) for k in range(2)]
    lines.append(pmix[:, ch:].T[:1, :])
    lines = stack(*lines, jnp.zeros((PIECE - 3, ch), F32))
    flat.append(beside(lines, jnp.zeros_like(lines)))
    for block in flat:
        for start in range(0, block.shape[0], PIECE):
            parcel[at] = block[start : start + PIECE, :].astype(BF16)
            at += 1
    for piece, (r, p) in enumerate(owners):
        home = r * parts + p

        @pl.when(me != home)
        def _():
            pltpu.make_async_remote_copy(
                src_ref=parcel.at[piece],
                dst_ref=slots.at[lax.rem(me - home + count, count) - 1],
                send_sem=send1,
                recv_sem=recv1,
                device_id=(r, p),
                device_id_type=MESH,
            ).start()

    def third(b, carry):
        for k, (side, t) in enumerate(sides):
            here = slice(t + OFF, t + OFF + EDGE)
            mask = tall(masks(b, t, EDGE), ch // 16)
            mid_grad = dot(wdt[...], stack(prep[b, :, here], pre[b, :, here], prem[b, :, here]))
            g = (bg[b, :, here].astype(F32) + mid_grad * slope[b, :, here]) * mask
            low = g.astype(BF16)
            if side == 0:
                put(gradm, b, t + OFF + 1, low)
            else:
                put(gradp, b, t + OFF - 1, low)
        for t in range(0, span, chunk):
            here = slice(t + OFF, t + OFF + chunk)
            there = slice(t, t + chunk)
            mask = masks(b, t, chunk, 2.0).astype(BF16)
            total = half[b, :, here] + dot(wm[...], gated[b, :, there]) + wide(biases[2], chunk // EDGE)
            outs[b, :, there] = total.astype(BF16) * tall(mask, ch // 16)
            low = masks(b, t, chunk).astype(BF16)
            dx = dot(wct[...], stack(gradm[b, :, here], grad[b, :, here], gradp[b, :, here]))
            dxs[b, :, there] = dx.astype(BF16) * tall(low, 2 * ch // 16)
        return carry

    lax.fori_loop(0, clips, third, 0)

    for piece, (r, p) in enumerate(owners):
        @pl.when(me == r * parts + p)
        def _():
            pltpu.make_async_copy(slots, slots, recv1).wait()
            total = parcel[piece].astype(F32)
            for k in range(count - 1):
                total = total + slots[k].astype(F32)
            total_ref[piece] = total.astype(BF16)
            others(
                lambda tr, tp: pltpu.make_async_remote_copy(
                    src_ref=total_ref.at[piece],
                    dst_ref=total_ref.at[piece],
                    send_sem=send2,
                    recv_sem=recv2,
                    device_id=(tr, tp),
                    device_id_type=MESH,
                ).start()
            )

    for side in range(2):
        @pl.when(has[side])
        def _():
            for move in moves(side):
                move.wait_send()
    owner = functools.reduce(jnp.logical_or, [me == r * parts + p for r, p in owners])

    @pl.when(owner)
    def _():
        rest = total_ref.at[pl.ds(0, pieces - 1)]
        pltpu.make_async_copy(rest, rest, recv2).wait()
        sent = parcel.at[pl.ds(0, pieces - 1)]
        pltpu.make_async_copy(sent, sent, send1).wait()
        pltpu.make_async_copy(slots, slots, send2).wait()

    @pl.when(jnp.logical_not(owner))
    def _():
        pltpu.make_async_copy(total_ref, total_ref, recv2).wait()
        pltpu.make_async_copy(parcel, parcel, send1).wait()


def layer_call(rows, parts, clips, span, pieces):
    ch = 64
    lanes = span + 4 * EDGE
    smem = pl.BlockSpec(memory_space=pltpu.SMEM)
    vmem = pl.BlockSpec(memory_space=pltpu.VMEM)
    hbm = pl.BlockSpec(memory_space=pl.ANY)
    low = pltpu.VMEM((clips, ch, lanes), BF16)
    high = pltpu.VMEM((clips, ch, lanes), F32)
    dma = pltpu.SemaphoreType.DMA
    return pl.pallas_call(
        functools.partial(layer, rows, parts, owner_list(rows, parts, pieces)),
        name="layer",
        in_specs=[smem, smem, hbm, hbm] + [vmem] * 6,
        out_specs=[vmem, vmem, vmem],
        out_shape=[
            pltpu.VMEM((clips, ch, span), BF16),
            pltpu.VMEM((clips, 2 * ch, span), BF16),
            pltpu.VMEM((pieces, PIECE, 2 * ch), BF16),
        ],
        scratch_shapes=[
            pltpu.VMEM((ch, 4 * ch), BF16),
            pltpu.VMEM((ch, 3 * ch), BF16),
            pltpu.VMEM((ch, ch), BF16),
            pltpu.VMEM((ch, ch), BF16),
            pltpu.VMEM((ch, 3 * ch), BF16),
            pltpu.VMEM((2 * ch, 3 * ch), BF16),
            pltpu.VMEM((3, ch, EDGE), F32),
        ]
        + [low] * 5
        + [high] * 2
        + [low] * 3
        + [pltpu.VMEM((clips, ch, span), BF16)]
        + [low] * 6
        + [
            pltpu.VMEM((2, clips, 2 * ch, EDGE), BF16),
            pltpu.VMEM((2, clips, ch, EDGE), BF16),
            pltpu.VMEM((2 * ch, 2 * ch), F32),
            pltpu.VMEM((2 * ch, 2 * ch), F32),
            pltpu.VMEM((ch, 2 * ch), F32),
            pltpu.VMEM((2, ch, EDGE), F32),
            pltpu.VMEM((pieces, PIECE, 2 * ch), BF16),
            pltpu.VMEM((rows * parts - 1, PIECE, 2 * ch), BF16),
            dma((clips, 3)),
            dma((2, 2)),
            dma((2, 2)),
            dma,
            dma,
            dma,
            dma,
        ],
        compiler_params=pltpu.CompilerParams(collective_id=0, has_side_effects=True, vmem_limit_bytes=54 << 20),
    )


def hand_over(out_in, clips_in, sums, out, clips, cg, cb, dg, db, mg, mb, sem):
    ch = 64
    moves = []
    for b in range(out.shape[0]):
        for k, (src, dst) in enumerate(((out_in, out), (clips_in, clips))):
            moves.append(pltpu.make_async_copy(src.at[b], dst.at[b], sem.at[b, k]))
    for move in moves:
        move.start()
    at = lambda start, count: sums[start : start + count, :].astype(F32)
    low, high = at(0, ch), at(ch, ch)
    for k, block in enumerate((low[:, :ch], low[:, ch:], high[:, :ch], high[:, ch:])):
        cg[:, k, :] = block
    block = at(2 * ch, ch)
    dg[1] = block[:, :ch]
    dg[0] = block[:, ch:]
    block = at(3 * ch, ch)
    dg[2] = block[:, :ch]
    mg[...] = block[:, ch:]
    lines = at(4 * ch, 16)[:, :ch]
    for k, ref in enumerate((cb, db, mb)):
        ref[...] = lines[k : k + 1]
    for move in moves:
        move.wait()


def hand_over_call(out, clips):
    ch = 64
    vmem = pl.BlockSpec(memory_space=pltpu.VMEM)
    hbm = pl.BlockSpec(memory_space=pl.ANY)
    shapes = [(ch, 4, ch), (1, ch), (3, ch, ch), (1, ch), (ch, ch), (1, ch)]
    like = lambda a: jax.ShapeDtypeStruct(a.shape, a.dtype)
    return pl.pallas_call(
        hand_over,
        name="hand_over",
        in_specs=[vmem, vmem, vmem],
        out_specs=[hbm, hbm] + [vmem] * 6,
        out_shape=[like(out), like(clips)] + [jax.ShapeDtypeStruct(s, F32) for s in shapes],
        scratch_shapes=[pltpu.SemaphoreType.DMA((out.shape[0], 2))],
        compiler_params=pltpu.CompilerParams(vmem_limit_bytes=8 << 20),
    )


def body(rows, parts, clips_in, cw, cb, dw, db, mw, mb, counts, groups, out_grad):
    clips, ch, span = out_grad.shape
    pieces = -(-(4 * ch + 16) // PIECE)
    layer_out, clips_grad, sums = layer_call(rows, parts, clips, span, pieces)(
        counts, groups, clips_in, out_grad, cw.transpose(0, 2, 1), dw.transpose(2, 0, 1), mw, cb[None], db[None], mb[None]
    )
    layer_out, clips_grad, cg, cbg, dg, dbg, mg, mbg = hand_over_call(layer_out, clips_grad)(
        layer_out, clips_grad, sums.reshape(pieces * PIECE, 2 * ch)
    )
    return (layer_out, clips_grad, cg.transpose(0, 2, 1), cbg[0], dg.transpose(1, 2, 0), dbg[0], mg, mbg[0])


def solution(mesh):
    split = P("batch", None, "tm")
    placed = (split, P(), P(), P(), P(), P(), P(), P("batch"), P("batch"), split)
    return jax.shard_map(
        functools.partial(body, mesh.shape["batch"], mesh.shape["tm"]),
        mesh=mesh,
        in_specs=placed,
        out_specs=(split, split) + (P(),) * 6,
        check_vma=False,
    )
```

```python
import functools

import jax
import jax.numpy as jnp
from jax import lax
from jax.experimental import pallas as pl
from jax.experimental.pallas import tpu as pltpu
from jax.sharding import PartitionSpec as P

DILATION = 27
EDGE = 128
OFF = 2 * EDGE
CHUNK = 2048
PIECE = 32
MESH = pl.DeviceIdType.MESH
F32 = jnp.float32
BF16 = jnp.bfloat16
C0 = 0.7978845608028654
C1 = 0.044715


def dot(a, b):
    return lax.dot_general(a, b, (((1,), (0,)), ((), ())), preferred_element_type=F32)


def dot_t(a, b):
    return lax.dot_general(a, b, (((1,), (1,)), ((), ())), preferred_element_type=F32)


def stack(*rows):
    return jnp.concatenate(rows, axis=0)


def beside(*parts):
    return jnp.concatenate(parts, axis=1)


def gelu_parts(half):
    square = half * half
    t = jnp.tanh(half * (2 * C0 + (8 * C0 * C1) * square))
    up = 1.0 + t
    value = half * up
    return value, up + (value * (1.0 - t)) * (2 * C0 + (24 * C0 * C1) * square)


def tall(rows, copies):
    return jnp.concatenate([rows] * copies, axis=0)


def wide(tile, count):
    return jnp.concatenate([tile] * count, axis=1)


def lane_groups(value):
    total = value[:, :EDGE]
    for start in range(EDGE, value.shape[1], EDGE):
        total = total + value[:, start : start + EDGE]
    return total


def owner_list(rows, parts, pieces):
    half = parts // 2
    order = sorted(range(half), key=lambda q: abs(2 * q - half + 1))
    spots = [(r, 2 * q + 1) for q in order for r in range(rows)]
    spots += [(r, 2 * q) for q in order for r in range(rows)]
    return spots[:pieces]


def layer(
    rows,
    parts,
    owners,
    counts,
    groups,
    x_ref,
    og_ref,
    cw,
    dw,
    mw,
    cb,
    db,
    mb,
    outs,
    dxs,
    total_ref,
    wc,
    wd,
    wm,
    wdt,
    wct,
    biases,
    x0,
    x1,
    bg,
    x0p,
    x1m,
    half,
    slope,
    mid,
    midm,
    midp,
    gated,
    pre,
    prem,
    prep,
    grad,
    gradm,
    gradp,
    xh,
    ogh,
    pconv,
    pdil,
    pmix,
    psum,
    parcel,
    slots,
    in_sem,
    send,
    recv,
    send1,
    recv1,
    send2,
    recv2,
):
    ch = 64
    clips, _, span = og_ref.shape
    chunk = min(CHUNK, span)
    pieces = len(owners)
    count = rows * parts
    row, place = lax.axis_index("batch"), lax.axis_index("tm")
    me = row * parts + place
    base = place * span

    def others(action):
        def step(r, carry):
            target = lax.rem(me + r, count)
            action(target // parts, lax.rem(target, parts))
            return carry

        lax.fori_loop(1, count, step, 0)

    inside = pl.ds(OFF, span)

    def fetches(b):
        return [
            pltpu.make_async_copy(x_ref.at[b, pl.ds(0, ch)], x0.at[b, :, inside], in_sem.at[b, 0]),
            pltpu.make_async_copy(x_ref.at[b, pl.ds(ch, ch)], x1.at[b, :, inside], in_sem.at[b, 1]),
            pltpu.make_async_copy(og_ref.at[b], bg.at[b, :, inside], in_sem.at[b, 2]),
        ]

    for b in range(clips):
        for fetch in fetches(b):
            fetch.start()
    xh[...] = jnp.zeros(xh.shape, BF16)
    ogh[...] = jnp.zeros(ogh.shape, BF16)
    barrier = pltpu.get_barrier_semaphore()
    others(lambda r, p: pl.semaphore_signal(barrier, inc=1, device_id=(r, p), device_id_type=MESH))

    flip = lambda w: w.astype(F32).T.astype(BF16)
    taps = [cw[:, k, :] for k in range(4)]
    zero = jnp.zeros((ch, ch), BF16)
    for k in range(4):
        wc[:, k * ch : (k + 1) * ch] = taps[k] * 0.5
    for k in range(3):
        wd[:ch, k * ch : (k + 1) * ch] = dw[k] * 0.5
        wd[ch:, k * ch : (k + 1) * ch] = zero
        wdt[:, k * ch : (k + 1) * ch] = flip(dw[k]) * 0.5
    wm[...] = mw[...] * 0.5
    wd[:ch, 3 * ch :] = zero
    wd[ch:, 3 * ch :] = flip(mw[...]) * 0.5
    back = [flip(tap) for tap in taps]
    wct[:ch, :] = beside(back[3], back[1], zero)
    wct[ch:, :] = beside(zero, back[2], back[0])
    for k, line in enumerate((cb, db, mb)):
        biases[k] = jnp.broadcast_to(line[...] * 0.5, (EDGE, ch)).T

    for ref, at in ((gradm, OFF), (gradm, OFF + span), (grad, OFF + span)):
        ref[:, :, at : at + EDGE] = jnp.zeros((clips, ch, EDGE), BF16)
    for ref in (pconv, pdil, pmix, psum):
        ref[...] = jnp.zeros(ref.shape, F32)

    def masks(b, t, n, high=1.0):
        valid = jnp.minimum(lax.shift_right_logical(counts[b], groups[b]), span * parts)
        frame = base + t + lax.broadcasted_iota(jnp.int32, (16, n), 1)
        return jnp.where((frame >= 0) & (frame < valid), high, 0.0)

    def put(ref, b, start, value):
        ref[b, :, start : start + value.shape[1]] = value

    has = (place > 0, place < parts - 1)
    other = (place - 1, place + 1)

    def moves(side):
        cut = pl.ds(0, EDGE) if side == 0 else pl.ds(span - EDGE, EDGE)
        return [
            pltpu.make_async_remote_copy(
                src_ref=src.at[:, :, cut],
                dst_ref=dst.at[1 - side],
                send_sem=send.at[side, k],
                recv_sem=recv.at[1 - side, k],
                device_id=(row, other[side]),
                device_id_type=MESH,
            )
            for k, (src, dst) in enumerate(((x_ref, xh), (og_ref, ogh)))
        ]

    def spot(t, n):
        return slice(t + OFF, t + OFF + n)

    def gather(ref, where):
        return beside(*[ref[b, :, spot(t, n)] for b, t, n in where])

    def cuts(where):
        at = 0
        for b, t, n in where:
            yield b, t, n, slice(at, at + n)
            at += n

    def spread(refs, where, step, low):
        now, before, after = refs
        for b, t, n, cut in cuts(where):
            now[b, :, spot(t, n)] = low[:, cut]
            put(before, b, t + OFF + step, low[:, cut])
            put(after, b, t + OFF - step, low[:, cut])

    def lows(where):
        return beside(*[tall(masks(b, t, n).astype(BF16), ch // 16) for b, t, n in where])

    def stage0(b, t, n):
        here = spot(t, n)
        low = lows([(b, t, n)])
        even = x0[b, :, here] * low
        x0[b, :, here] = even
        put(x0p, b, t + OFF - 1, even)
        put(x1m, b, t + OFF + 1, x1[b, :, here])
        bg[b, :, here] = bg[b, :, here] * low

    def stage1(where):
        taps = stack(gather(x1m, where), gather(x0, where), gather(x1, where), gather(x0p, where))
        h = dot(wc[...], taps)
        h = h + wide(biases[0], h.shape[1] // EDGE)
        value, s = gelu_parts(h)
        for b, t, n, cut in cuts(where):
            half[b, :, spot(t, n)] = h[:, cut]
            slope[b, :, spot(t, n)] = s[:, cut]
        spread((mid, midm, midp), where, DILATION, value.astype(BF16) * lows(where))

    def own(where):
        kept = [(b, max(t, 0), min(t + n, span) - max(t, 0)) for b, t, n in where]
        return kept, [
            slice(cut.start + kt - t, cut.start + kt - t + kn)
            for (b, t, n, cut), (_, kt, kn) in zip(cuts(where), kept)
        ]

    def stage2(where):
        taps = stack(gather(midm, where), gather(mid, where), gather(midp, where), gather(bg, where))
        both = dot(wd[...], taps)
        d = both[:ch] + wide(biases[1], both.shape[1] // EDGE)
        value, s = gelu_parts(d)
        pg = both[ch:] * s
        spread((pre, prem, prep), where, DILATION, pg.astype(BF16))
        kept, inner = own(where)
        low = value.astype(BF16)
        for (b, t, n), cut in zip(kept, inner):
            gated[b, :, t : t + n] = low[:, cut]
            psum[1] += lane_groups(pg[:, cut])
        low = beside(*[low[:, cut] for cut in inner])
        ones = jnp.ones((16, low.shape[1]), BF16)
        pmix[:, : ch + 16] += dot_t(gather(bg, kept), stack(low, ones))

    def stage3(where, halo=False):
        mid_grad = dot(wdt[...], stack(gather(prep, where), gather(pre, where), gather(prem, where)))
        mask = beside(*[tall(masks(b, t, n), ch // 16) for b, t, n in where])
        g = (gather(bg, where).astype(F32) + mid_grad * gather(slope, where)) * mask
        low = g.astype(BF16)
        kept, inner = own(where)
        for (b, t, n), cut in zip(kept, inner):
            psum[0] += lane_groups(g[:, cut])
            spread((grad, gradm, gradp), [(b, t, n)], 1, low[:, cut])
        return low

    def dilated_sums(where):
        pdil[...] += dot_t(
            stack(gather(pre, where), gather(prem, where)), stack(gather(mid, where), gather(midm, where))
        )

    def strided_sums(where):
        pconv[...] += dot_t(
            stack(gather(grad, where), gather(gradm, where)), stack(gather(x1m, where), gather(x0, where))
        )

    def pieces_of(b, margin):
        edges = [margin] + list(range(chunk, span - margin, chunk)) + [span - margin]
        return [(b, t, e - t) for t, e in zip(edges, edges[1:])]

    def first(b):
        def start():
            for fetch in fetches(b):
                fetch.wait()
            for t in range(0, span, chunk):
                stage0(b, t, chunk)

        return [start] + [functools.partial(stage1, [piece]) for piece in pieces_of(b, EDGE)]

    def later(piece):
        b, t, n = piece
        skip = EDGE if t == 3 * EDGE else 0
        return b, t + skip, n - skip

    def second(b):
        work = [functools.partial(stage2, [piece]) for piece in pieces_of(b, 2 * EDGE)]
        for piece in pieces_of(b, 3 * EDGE):
            work += [
                functools.partial(stage3, [piece]),
                functools.partial(dilated_sums, [piece]),
                functools.partial(strided_sums, [later(piece)]),
            ]
        return work

    def run(work):
        for step in work:
            step()

    run(first(0))
    pl.semaphore_wait(barrier, count - 1)
    for side in range(2):
        @pl.when(has[side])
        def _():
            for move in moves(side):
                move.start()
    for b in range(clips):
        work, ahead = second(b), first(b + 1) if b + 1 < clips else []
        order = []
        while work or ahead:
            order += work[:2] + ahead[:1]
            work, ahead = work[2:], ahead[1:]
        run(order)

    for side in range(2):
        @pl.when(has[side])
        def _():
            for move in moves(1 - side):
                move.wait_recv()

    def edge(width):
        return [
            (b, -EDGE if side == 0 else span - width, width + EDGE) for b in range(clips) for side in range(2)
        ]

    for b, t, n in edge(0):
        side = 0 if t < 0 else 1
        low = lows([(b, t, n)])
        even = xh[side, b, :ch] * low
        odd = xh[side, b, ch:]
        x0[b, :, spot(t, n)] = even
        x1[b, :, spot(t, n)] = odd
        put(x0p, b, t + OFF - 1, even)
        put(x1m, b, t + OFF + 1, odd)
        bg[b, :, spot(t, n)] = ogh[side, b] * low
    stage1(edge(EDGE))
    stage2(edge(2 * EDGE))
    low = stage3(edge(3 * EDGE))
    dilated_sums(own(edge(3 * EDGE))[0])
    strided_sums([(b, max(t, 0), 4 * EDGE) for b, t, _ in edge(3 * EDGE)])
    for b, t, n, cut in cuts(edge(3 * EDGE)):
        if t < 0:
            put(gradm, b, t + OFF + 1, low[:, cut.start : cut.start + EDGE])
        else:
            put(gradp, b, span + OFF - 1, low[:, cut.stop - EDGE : cut.stop])

    at = 0
    flat = [
        pconv[...],
        pdil[:ch, :],
        beside(pdil[ch:, :ch], pmix[:, :ch]),
    ]
    lines = [jnp.sum(psum[k].T, axis=0, keepdims=True) for k in range(2)]
    lines.append(pmix[:, ch:].T[:1, :])
    lines = stack(*lines, jnp.zeros((PIECE - 3, ch), F32))
    flat.append(beside(lines, jnp.zeros_like(lines)))
    for block in flat:
        for start in range(0, block.shape[0], PIECE):
            parcel[at] = block[start : start + PIECE, :].astype(BF16)
            at += 1
    for piece, (r, p) in enumerate(owners):
        home = r * parts + p

        @pl.when(me != home)
        def _():
            pltpu.make_async_remote_copy(
                src_ref=parcel.at[piece],
                dst_ref=slots.at[lax.rem(me - home + count, count) - 1],
                send_sem=send1,
                recv_sem=recv1,
                device_id=(r, p),
                device_id_type=MESH,
            ).start()

    def third(b, carry):
        for t in range(0, span, chunk):
            here = slice(t + OFF, t + OFF + chunk)
            there = slice(t, t + chunk)
            mask = masks(b, t, chunk, 2.0).astype(BF16)
            total = half[b, :, here] + dot(wm[...], gated[b, :, there]) + wide(biases[2], chunk // EDGE)
            outs[b, :, there] = total.astype(BF16) * tall(mask, ch // 16)
            low = masks(b, t, chunk).astype(BF16)
            dx = dot(wct[...], stack(gradm[b, :, here], grad[b, :, here], gradp[b, :, here]))
            dxs[b, :, there] = dx.astype(BF16) * tall(low, 2 * ch // 16)
        return carry

    lax.fori_loop(0, clips, third, 0)

    for piece, (r, p) in enumerate(owners):
        @pl.when(me == r * parts + p)
        def _():
            pltpu.make_async_copy(slots, slots, recv1).wait()
            total = parcel[piece].astype(F32)
            for k in range(count - 1):
                total = total + slots[k].astype(F32)
            total_ref[piece] = total.astype(BF16)
            others(
                lambda tr, tp: pltpu.make_async_remote_copy(
                    src_ref=total_ref.at[piece],
                    dst_ref=total_ref.at[piece],
                    send_sem=send2,
                    recv_sem=recv2,
                    device_id=(tr, tp),
                    device_id_type=MESH,
                ).start()
            )

    for side in range(2):
        @pl.when(has[side])
        def _():
            for move in moves(side):
                move.wait_send()
    owner = functools.reduce(jnp.logical_or, [me == r * parts + p for r, p in owners])

    @pl.when(owner)
    def _():
        rest = total_ref.at[pl.ds(0, pieces - 1)]
        pltpu.make_async_copy(rest, rest, recv2).wait()
        sent = parcel.at[pl.ds(0, pieces - 1)]
        pltpu.make_async_copy(sent, sent, send1).wait()
        pltpu.make_async_copy(slots, slots, send2).wait()

    @pl.when(jnp.logical_not(owner))
    def _():
        pltpu.make_async_copy(total_ref, total_ref, recv2).wait()
        pltpu.make_async_copy(parcel, parcel, send1).wait()


def layer_call(rows, parts, clips, span, pieces):
    ch = 64
    lanes = span + 4 * EDGE
    smem = pl.BlockSpec(memory_space=pltpu.SMEM)
    vmem = pl.BlockSpec(memory_space=pltpu.VMEM)
    hbm = pl.BlockSpec(memory_space=pl.ANY)
    low = pltpu.VMEM((clips, ch, lanes), BF16)
    high = pltpu.VMEM((clips, ch, lanes), F32)
    dma = pltpu.SemaphoreType.DMA
    return pl.pallas_call(
        functools.partial(layer, rows, parts, owner_list(rows, parts, pieces)),
        name="layer",
        in_specs=[smem, smem, hbm, hbm] + [vmem] * 6,
        out_specs=[vmem, vmem, vmem],
        out_shape=[
            pltpu.VMEM((clips, ch, span), BF16),
            pltpu.VMEM((clips, 2 * ch, span), BF16),
            pltpu.VMEM((pieces, PIECE, 2 * ch), BF16),
        ],
        scratch_shapes=[
            pltpu.VMEM((ch, 4 * ch), BF16),
            pltpu.VMEM((2 * ch, 4 * ch), BF16),
            pltpu.VMEM((ch, ch), BF16),
            pltpu.VMEM((ch, 3 * ch), BF16),
            pltpu.VMEM((2 * ch, 3 * ch), BF16),
            pltpu.VMEM((3, ch, EDGE), F32),
        ]
        + [low] * 5
        + [high] * 2
        + [low] * 3
        + [pltpu.VMEM((clips, ch, span), BF16)]
        + [low] * 6
        + [
            pltpu.VMEM((2, clips, 2 * ch, EDGE), BF16),
            pltpu.VMEM((2, clips, ch, EDGE), BF16),
            pltpu.VMEM((2 * ch, 2 * ch), F32),
            pltpu.VMEM((2 * ch, 2 * ch), F32),
            pltpu.VMEM((ch, 2 * ch), F32),
            pltpu.VMEM((2, ch, EDGE), F32),
            pltpu.VMEM((pieces, PIECE, 2 * ch), BF16),
            pltpu.VMEM((rows * parts - 1, PIECE, 2 * ch), BF16),
            dma((clips, 3)),
            dma((2, 2)),
            dma((2, 2)),
            dma,
            dma,
            dma,
            dma,
        ],
        compiler_params=pltpu.CompilerParams(collective_id=0, has_side_effects=True, vmem_limit_bytes=54 << 20),
    )


def hand_over(out_in, clips_in, sums, out, clips, cg, cb, dg, db, mg, mb, sem):
    ch = 64
    moves = []
    for b in range(out.shape[0]):
        for k, (src, dst) in enumerate(((out_in, out), (clips_in, clips))):
            moves.append(pltpu.make_async_copy(src.at[b], dst.at[b], sem.at[b, k]))
    for move in moves:
        move.start()
    at = lambda start, count: sums[start : start + count, :].astype(F32)
    low, high = at(0, ch), at(ch, ch)
    for k, block in enumerate((low[:, :ch], low[:, ch:], high[:, :ch], high[:, ch:])):
        cg[:, k, :] = block
    block = at(2 * ch, ch)
    dg[1] = block[:, :ch]
    dg[0] = block[:, ch:]
    block = at(3 * ch, ch)
    dg[2] = block[:, :ch]
    mg[...] = block[:, ch:]
    lines = at(4 * ch, 16)[:, :ch]
    for k, ref in enumerate((cb, db, mb)):
        ref[...] = lines[k : k + 1]
    for move in moves:
        move.wait()


def hand_over_call(out, clips):
    ch = 64
    vmem = pl.BlockSpec(memory_space=pltpu.VMEM)
    hbm = pl.BlockSpec(memory_space=pl.ANY)
    shapes = [(ch, 4, ch), (1, ch), (3, ch, ch), (1, ch), (ch, ch), (1, ch)]
    like = lambda a: jax.ShapeDtypeStruct(a.shape, a.dtype)
    return pl.pallas_call(
        hand_over,
        name="hand_over",
        in_specs=[vmem, vmem, vmem],
        out_specs=[hbm, hbm] + [vmem] * 6,
        out_shape=[like(out), like(clips)] + [jax.ShapeDtypeStruct(s, F32) for s in shapes],
        scratch_shapes=[pltpu.SemaphoreType.DMA((out.shape[0], 2))],
        compiler_params=pltpu.CompilerParams(vmem_limit_bytes=8 << 20),
    )


def body(rows, parts, clips_in, cw, cb, dw, db, mw, mb, counts, groups, out_grad):
    clips, ch, span = out_grad.shape
    pieces = -(-(4 * ch + 16) // PIECE)
    layer_out, clips_grad, sums = layer_call(rows, parts, clips, span, pieces)(
        counts, groups, clips_in, out_grad, cw.transpose(0, 2, 1), dw.transpose(2, 0, 1), mw, cb[None], db[None], mb[None]
    )
    layer_out, clips_grad, cg, cbg, dg, dbg, mg, mbg = hand_over_call(layer_out, clips_grad)(
        layer_out, clips_grad, sums.reshape(pieces * PIECE, 2 * ch)
    )
    return (layer_out, clips_grad, cg.transpose(0, 2, 1), cbg[0], dg.transpose(1, 2, 0), dbg[0], mg, mbg[0])


def solution(mesh):
    split = P("batch", None, "tm")
    placed = (split, P(), P(), P(), P(), P(), P(), P("batch"), P("batch"), split)
    return jax.shard_map(
        functools.partial(body, mesh.shape["batch"], mesh.shape["tm"]),
        mesh=mesh,
        in_specs=placed,
        out_specs=(split, split) + (P(),) * 6,
        check_vma=False,
    )
```

```python
import functools

import jax
import jax.numpy as jnp
from jax import lax
from jax.experimental import pallas as pl
from jax.experimental.pallas import tpu as pltpu
from jax.sharding import PartitionSpec as P

DILATION = 27
EDGE = 128
OFF = 2 * EDGE
CHUNK = 4096
SUB = 256
SUMS = 1024
RATIO = 2
PIECE = 32
MESH = pl.DeviceIdType.MESH
F32 = jnp.float32
BF16 = jnp.bfloat16
C0 = 0.7978845608028654
C1 = 0.044715


def dot(a, b):
    return lax.dot_general(a, b, (((1,), (0,)), ((), ())), preferred_element_type=F32)


def dot_t(a, b):
    return lax.dot_general(a, b, (((1,), (1,)), ((), ())), preferred_element_type=F32)


def stack(*rows):
    return jnp.concatenate(rows, axis=0)


def beside(*parts):
    return jnp.concatenate(parts, axis=1)


def gelu_parts(half):
    square = half * half
    t = jnp.tanh(half * (2 * C0 + (8 * C0 * C1) * square))
    up = 1.0 + t
    value = half * up
    return value, up + (value * (1.0 - t)) * (2 * C0 + (24 * C0 * C1) * square)


def tall(rows, copies):
    return jnp.concatenate([rows] * copies, axis=0)


def wide(tile, count):
    return jnp.concatenate([tile] * count, axis=1)


def lane_groups(value):
    total = value[:, :EDGE]
    for start in range(EDGE, value.shape[1], EDGE):
        total = total + value[:, start : start + EDGE]
    return total


def owner_list(rows, parts, pieces):
    half = parts // 2
    order = sorted(range(half), key=lambda q: abs(2 * q - half + 1))
    spots = [(r, 2 * q + 1) for q in order for r in range(rows)]
    spots += [(r, 2 * q) for q in order for r in range(rows)]
    return spots[:pieces]


def layer(
    rows,
    parts,
    owners,
    counts_ref,
    groups_ref,
    x_ref,
    og_ref,
    cw_ref,
    dw_ref,
    mw_ref,
    cb_ref,
    db_ref,
    mb_ref,
    outs,
    dxs,
    total_ref,
    wc,
    wd,
    wm,
    wdt,
    wct,
    biases,
    x0,
    x1,
    bg,
    x0p,
    x1m,
    half,
    slope,
    mid,
    midm,
    midp,
    gated,
    pre,
    prem,
    prep,
    grad,
    gradm,
    gradp,
    xh,
    ogh,
    pconv,
    pdil,
    pmix,
    psum,
    parcel,
    slots,
    counts,
    groups,
    cw,
    dw,
    mw,
    cb,
    db,
    mb,
    small_sem,
    in_sem,
    send,
    recv,
    send1,
    recv1,
    send2,
    recv2,
):
    ch = 64
    clips, _, span = og_ref.shape
    chunk = min(CHUNK, span)
    pieces = len(owners)
    count = rows * parts
    row, place = lax.axis_index("batch"), lax.axis_index("tm")
    me = row * parts + place
    base = place * span

    def others(action):
        def step(r, carry):
            target = lax.rem(me + r, count)
            action(target // parts, lax.rem(target, parts))
            return carry

        lax.fori_loop(1, count, step, 0)

    inside = pl.ds(OFF, span)

    def fetches(b):
        return [
            pltpu.make_async_copy(x_ref.at[b, pl.ds(0, ch)], x0.at[b, :, inside], in_sem.at[b, 0]),
            pltpu.make_async_copy(x_ref.at[b, pl.ds(ch, ch)], x1.at[b, :, inside], in_sem.at[b, 1]),
            pltpu.make_async_copy(og_ref.at[b], bg.at[b, :, inside], in_sem.at[b, 2]),
        ]

    small = [
        pltpu.make_async_copy(src, dst, small_sem.at[k])
        for k, (src, dst) in enumerate(
            (
                (cw_ref, cw),
                (dw_ref, dw),
                (mw_ref, mw),
                (cb_ref, cb),
                (db_ref, db),
                (mb_ref, mb),
                (counts_ref, counts),
                (groups_ref, groups),
            )
        )
    ]
    for fetch in small + fetches(0) + fetches(1):
        fetch.start()
    xh[...] = jnp.zeros(xh.shape, BF16)
    ogh[...] = jnp.zeros(ogh.shape, BF16)
    barrier = pltpu.get_barrier_semaphore()
    others(lambda r, p: pl.semaphore_signal(barrier, inc=1, device_id=(r, p), device_id_type=MESH))

    for fetch in small:
        fetch.wait()
    flip = lambda w: w.astype(F32).T.astype(BF16)
    taps = [cw[:, k, :] for k in range(4)]
    zero = jnp.zeros((ch, ch), BF16)
    for k in range(4):
        wc[:, k * ch : (k + 1) * ch] = taps[k] * 0.5
    for k in range(3):
        wd[:ch, k * ch : (k + 1) * ch] = dw[k] * 0.5
        wd[ch:, k * ch : (k + 1) * ch] = zero
        wdt[:, k * ch : (k + 1) * ch] = flip(dw[k]) * 0.5
    wm[...] = mw[...] * 0.5
    wd[:ch, 3 * ch :] = zero
    wd[ch:, 3 * ch :] = flip(mw[...]) * 0.5
    back = [flip(tap) for tap in taps]
    wct[:ch, :] = beside(back[3], back[1], zero)
    wct[ch:, :] = beside(zero, back[2], back[0])
    for k, line in enumerate((cb, db, mb)):
        biases[k] = jnp.broadcast_to(line[...] * 0.5, (EDGE, ch)).T

    for ref, at in ((gradm, OFF), (gradm, OFF + span), (grad, OFF + span)):
        ref[:, :, at : at + EDGE] = jnp.zeros((clips, ch, EDGE), BF16)
    for ref in (pconv, pdil, pmix, psum):
        ref[...] = jnp.zeros(ref.shape, F32)

    def masks(b, t, n, high=1.0):
        valid = jnp.minimum(lax.shift_right_logical(counts[b], groups[b]), span * parts)
        frame = base + t + lax.broadcasted_iota(jnp.int32, (16, n), 1)
        return jnp.where((frame >= 0) & (frame < valid), high, 0.0)

    def put(ref, b, start, value):
        ref[b, :, start : start + value.shape[1]] = value

    has = (place > 0, place < parts - 1)
    other = (place - 1, place + 1)

    def moves(side):
        cut = pl.ds(0, EDGE) if side == 0 else pl.ds(span - EDGE, EDGE)
        return [
            pltpu.make_async_remote_copy(
                src_ref=src.at[:, :, cut],
                dst_ref=dst.at[1 - side],
                send_sem=send.at[side, k],
                recv_sem=recv.at[1 - side, k],
                device_id=(row, other[side]),
                device_id_type=MESH,
            )
            for k, (src, dst) in enumerate(((x_ref, xh), (og_ref, ogh)))
        ]

    def spot(t, n):
        return slice(t + OFF, t + OFF + n)

    def gather(ref, where):
        return beside(*[ref[b, :, spot(t, n)] for b, t, n in where])

    def cuts(where):
        at = 0
        for b, t, n in where:
            yield b, t, n, slice(at, at + n)
            at += n

    def spread(refs, where, step, low):
        now, before, after = refs
        for b, t, n, cut in cuts(where):
            now[b, :, spot(t, n)] = low[:, cut]
            put(before, b, t + OFF + step, low[:, cut])
            put(after, b, t + OFF - step, low[:, cut])

    def lows(where):
        return beside(*[tall(masks(b, t, n).astype(BF16), ch // 16) for b, t, n in where])

    def stage0(b, t, n):
        here = spot(t, n)
        low = lows([(b, t, n)])
        even = x0[b, :, here] * low
        x0[b, :, here] = even
        put(x0p, b, t + OFF - 1, even)
        put(x1m, b, t + OFF + 1, x1[b, :, here])
        bg[b, :, here] = bg[b, :, here] * low

    def tiles(where):
        found = []
        for b, t, n, cut in cuts(where):
            at = t
            while at < t + n:
                stop = min([at + SUB, t + n] + [border for border in (0, span) if border > at])
                found.append(((b, at, stop - at), slice(cut.start + at - t, cut.start + stop - t)))
                at = stop
        return found

    def stage1(where):
        taps = stack(gather(x1m, where), gather(x0, where), gather(x1, where), gather(x0p, where))
        product = dot(wc[...], taps)
        yield
        for (b, t, n), cut in tiles(where):
            h = product[:, cut] + wide(biases[0], n // EDGE)
            value, s = gelu_parts(h)
            half[b, :, spot(t, n)] = h
            slope[b, :, spot(t, n)] = s
            spread((mid, midm, midp), [(b, t, n)], DILATION, value.astype(BF16) * lows([(b, t, n)]))
            yield

    def own(where):
        kept = [(b, max(t, 0), min(t + n, span) - max(t, 0)) for b, t, n in where]
        return kept, [
            slice(cut.start + kt - t, cut.start + kt - t + kn)
            for (b, t, n, cut), (_, kt, kn) in zip(cuts(where), kept)
        ]

    def inside_of(t, n):
        return 0 <= t and t + n <= span

    def stage2(where):
        taps = stack(gather(midm, where), gather(mid, where), gather(midp, where), gather(bg, where))
        both = dot(wd[...], taps)
        yield
        lows_of, kept = [], []
        for (b, t, n), cut in tiles(where):
            d = both[:ch, cut] + wide(biases[1], n // EDGE)
            value, s = gelu_parts(d)
            pg = both[ch:, cut] * s
            spread((pre, prem, prep), [(b, t, n)], DILATION, pg.astype(BF16))
            if inside_of(t, n):
                low = value.astype(BF16)
                gated[b, :, t : t + n] = low
                psum[1] += lane_groups(pg)
                lows_of.append(low)
                kept.append((b, t, n))
            yield
        low = beside(*lows_of)
        pmix[:, : ch + 16] += dot_t(gather(bg, kept), stack(low, jnp.ones((16, low.shape[1]), BF16)))
        yield

    def stage3(where, halo=None):
        mid_grad = dot(wdt[...], stack(gather(prep, where), gather(pre, where), gather(prem, where)))
        yield
        for (b, t, n), cut in tiles(where):
            mask = tall(masks(b, t, n), ch // 16)
            here = spot(t, n)
            g = (bg[b, :, here].astype(F32) + mid_grad[:, cut] * slope[b, :, here]) * mask
            low = g.astype(BF16)
            if inside_of(t, n):
                psum[0] += lane_groups(g)
                spread((grad, gradm, gradp), [(b, t, n)], 1, low)
            elif halo is not None:
                halo.append((b, t, low))
            yield

    def by_steps(sums, where):
        for b, t, n in where:
            for k in range(0, n, SUMS):
                sums([(b, t + k, min(SUMS, n - k))])
                yield

    def dilated_sums(where):
        pdil[...] += dot_t(
            stack(gather(pre, where), gather(prem, where)), stack(gather(mid, where), gather(midm, where))
        )

    def strided_sums(where):
        pconv[...] += dot_t(
            stack(gather(grad, where), gather(gradm, where)), stack(gather(x1m, where), gather(x0, where))
        )

    def pieces_of(b, margin):
        edges = [margin] + list(range(chunk, span - margin, chunk)) + [span - margin]
        return [(b, t, e - t) for t, e in zip(edges, edges[1:])]

    def first(b):
        for t in range(0, span, chunk):
            stage0(b, t, chunk)
            yield
        for piece in pieces_of(b, EDGE):
            yield from stage1([piece])

    def later(piece):
        b, t, n = piece
        skip = EDGE if t == 3 * EDGE else 0
        return b, t + skip, n - skip

    def second(b):
        for piece in pieces_of(b, 2 * EDGE):
            yield from stage2([piece])
        for piece in pieces_of(b, 3 * EDGE):
            yield from stage3([piece])
            yield from by_steps(dilated_sums, [piece])
            yield from by_steps(strided_sums, [later(piece)])

    def mix(main, side, ratio):
        done = object()
        while True:
            ended = [next(main, done) is done for _ in range(ratio)]
            if next(side, done) is done and ended[-1]:
                return

    def run(work):
        for _ in work:
            pass

    def edge(width):
        return [
            (b, -EDGE if side == 0 else span - width, width + EDGE) for b in range(clips) for side in range(2)
        ]

    def outside():
        for b, t, n in edge(0):
            side = 0 if t < 0 else 1
            low = lows([(b, t, n)])
            even = xh[side, b, :ch] * low
            odd = xh[side, b, ch:]
            x0[b, :, spot(t, n)] = even
            x1[b, :, spot(t, n)] = odd
            put(x0p, b, t + OFF - 1, even)
            put(x1m, b, t + OFF + 1, odd)
            bg[b, :, spot(t, n)] = ogh[side, b] * low
        yield
        yield from stage1(edge(EDGE))
        yield from stage2(edge(2 * EDGE))
        halo = []
        yield from stage3(edge(3 * EDGE), halo)
        dilated_sums(own(edge(3 * EDGE))[0])
        strided_sums([(b, max(t, 0), 4 * EDGE) for b, t, _ in edge(3 * EDGE)])
        for b, t, low in halo:
            if t < 0:
                put(gradm, b, t + OFF + 1, low)
            else:
                put(gradp, b, t + OFF - 1, low)
        yield

    def arrive(b):
        for fetch in fetches(b):
            fetch.wait()

    arrive(0)
    run(first(0))
    pl.semaphore_wait(barrier, count - 1)
    for side in range(2):
        @pl.when(has[side])
        def _():
            for move in moves(side):
                move.start()
    for b in range(clips - 1):
        arrive(b + 1)
        if b + 2 < clips:
            for fetch in fetches(b + 2):
                fetch.start()
        mix(second(b), first(b + 1), RATIO)

    for side in range(2):
        @pl.when(has[side])
        def _():
            for move in moves(1 - side):
                move.wait_recv()
    mix(second(clips - 1), outside(), RATIO)

    at = 0
    flat = [
        pconv[...],
        pdil[:ch, :],
        beside(pdil[ch:, :ch], pmix[:, :ch]),
    ]
    lines = [jnp.sum(psum[k].T, axis=0, keepdims=True) for k in range(2)]
    lines.append(pmix[:, ch:].T[:1, :])
    lines = stack(*lines, jnp.zeros((PIECE - 3, ch), F32))
    flat.append(beside(lines, jnp.zeros_like(lines)))
    for block in flat:
        for start in range(0, block.shape[0], PIECE):
            parcel[at] = block[start : start + PIECE, :].astype(BF16)
            at += 1
    for piece, (r, p) in enumerate(owners):
        home = r * parts + p

        @pl.when(me != home)
        def _():
            pltpu.make_async_remote_copy(
                src_ref=parcel.at[piece],
                dst_ref=slots.at[lax.rem(me - home + count, count) - 1],
                send_sem=send1,
                recv_sem=recv1,
                device_id=(r, p),
                device_id_type=MESH,
            ).start()

    def third(b, carry):
        for t in range(0, span, chunk):
            here = slice(t + OFF, t + OFF + chunk)
            there = slice(t, t + chunk)
            mask = masks(b, t, chunk, 2.0).astype(BF16)
            total = half[b, :, here] + dot(wm[...], gated[b, :, there]) + wide(biases[2], chunk // EDGE)
            outs[b, :, there] = total.astype(BF16) * tall(mask, ch // 16)
            low = masks(b, t, chunk).astype(BF16)
            dx = dot(wct[...], stack(gradm[b, :, here], grad[b, :, here], gradp[b, :, here]))
            dxs[b, :, there] = dx.astype(BF16) * tall(low, 2 * ch // 16)
        return carry

    lax.fori_loop(0, clips, third, 0)

    homes = [r * parts + p for r, p in owners]
    owner = functools.reduce(jnp.logical_or, [me == home for home in homes])
    mine = sum(jnp.where(me == home, piece, 0) for piece, home in enumerate(homes))

    @pl.when(owner)
    def _():
        pltpu.make_async_copy(slots, slots, recv1).wait()
        total = parcel[mine].astype(F32)
        for k in range(count - 1):
            total = total + slots[k].astype(F32)
        total_ref[mine] = total.astype(BF16)
        for k in range(1, count):
            target = lax.rem(me + k, count)
            pltpu.make_async_remote_copy(
                src_ref=total_ref.at[mine],
                dst_ref=total_ref.at[mine],
                send_sem=send2,
                recv_sem=recv2,
                device_id=(target // parts, lax.rem(target, parts)),
                device_id_type=MESH,
            ).start()

    for side in range(2):
        @pl.when(has[side])
        def _():
            for move in moves(side):
                move.wait_send()
    @pl.when(owner)
    def _():
        rest = total_ref.at[pl.ds(0, pieces - 1)]
        pltpu.make_async_copy(rest, rest, recv2).wait()
        sent = parcel.at[pl.ds(0, pieces - 1)]
        pltpu.make_async_copy(sent, sent, send1).wait()
        pltpu.make_async_copy(slots, slots, send2).wait()

    @pl.when(jnp.logical_not(owner))
    def _():
        pltpu.make_async_copy(total_ref, total_ref, recv2).wait()
        pltpu.make_async_copy(parcel, parcel, send1).wait()


def layer_call(rows, parts, clips, span, pieces):
    ch = 64
    lanes = span + 4 * EDGE
    vmem = pl.BlockSpec(memory_space=pltpu.VMEM)
    hbm = pl.BlockSpec(memory_space=pl.ANY)
    low = pltpu.VMEM((clips, ch, lanes), BF16)
    high = pltpu.VMEM((clips, ch, lanes), F32)
    dma = pltpu.SemaphoreType.DMA
    return pl.pallas_call(
        functools.partial(layer, rows, parts, owner_list(rows, parts, pieces)),
        name="layer",
        in_specs=[hbm] * 10,
        out_specs=[vmem, vmem, vmem],
        out_shape=[
            pltpu.VMEM((clips, ch, span), BF16),
            pltpu.VMEM((clips, 2 * ch, span), BF16),
            pltpu.VMEM((pieces, PIECE, 2 * ch), BF16),
        ],
        scratch_shapes=[
            pltpu.VMEM((ch, 4 * ch), BF16),
            pltpu.VMEM((2 * ch, 4 * ch), BF16),
            pltpu.VMEM((ch, ch), BF16),
            pltpu.VMEM((ch, 3 * ch), BF16),
            pltpu.VMEM((2 * ch, 3 * ch), BF16),
            pltpu.VMEM((3, ch, EDGE), F32),
        ]
        + [low] * 5
        + [high] * 2
        + [low] * 3
        + [pltpu.VMEM((clips, ch, span), BF16)]
        + [low] * 6
        + [
            pltpu.VMEM((2, clips, 2 * ch, EDGE), BF16),
            pltpu.VMEM((2, clips, ch, EDGE), BF16),
            pltpu.VMEM((2 * ch, 2 * ch), F32),
            pltpu.VMEM((2 * ch, 2 * ch), F32),
            pltpu.VMEM((ch, 2 * ch), F32),
            pltpu.VMEM((2, ch, EDGE), F32),
            pltpu.VMEM((pieces, PIECE, 2 * ch), BF16),
            pltpu.VMEM((rows * parts - 1, PIECE, 2 * ch), BF16),
            pltpu.SMEM((clips,), jnp.int32),
            pltpu.SMEM((clips,), jnp.int32),
            pltpu.VMEM((ch, 4, ch), BF16),
            pltpu.VMEM((3, ch, ch), BF16),
            pltpu.VMEM((ch, ch), BF16),
            pltpu.VMEM((1, ch), F32),
            pltpu.VMEM((1, ch), F32),
            pltpu.VMEM((1, ch), F32),
            dma((8,)),
            dma((clips, 3)),
            dma((2, 2)),
            dma((2, 2)),
            dma,
            dma,
            dma,
            dma,
        ],
        compiler_params=pltpu.CompilerParams(collective_id=0, has_side_effects=True, vmem_limit_bytes=54 << 20),
    )


def hand_over(out_in, clips_in, sums, *refs):
    out, clips = refs[:2]
    finals, (cg, cb, dg, db, mg, mb), (sem, small_sem) = refs[2:8], refs[8:14], refs[14:]
    ch = 64
    moves = []
    for b in range(out.shape[0]):
        for k, (src, dst) in enumerate(((out_in, out), (clips_in, clips))):
            moves.append(pltpu.make_async_copy(src.at[b], dst.at[b], sem.at[b, k]))
    for move in moves:
        move.start()
    at = lambda start, count: sums[start : start + count, :].astype(F32)
    low, high = at(0, ch), at(ch, ch)
    for k, block in enumerate((low[:, :ch], low[:, ch:], high[:, :ch], high[:, ch:])):
        cg[:, k, :] = block
    block = at(2 * ch, ch)
    dg[1] = block[:, :ch]
    dg[0] = block[:, ch:]
    block = at(3 * ch, ch)
    dg[2] = block[:, :ch]
    mg[...] = block[:, ch:]
    lines = at(4 * ch, 16)[:, :ch]
    for k, ref in enumerate((cb, db, mb)):
        ref[...] = lines[k : k + 1]
    for k, (src, dst) in enumerate(zip((cg, cb, dg, db, mg, mb), finals)):
        moves.append(pltpu.make_async_copy(src, dst, small_sem.at[k]))
        moves[-1].start()
    for move in moves:
        move.wait()


def hand_over_call(out, clips):
    ch = 64
    vmem = pl.BlockSpec(memory_space=pltpu.VMEM)
    hbm = pl.BlockSpec(memory_space=pl.ANY)
    shapes = [(ch, 4, ch), (1, ch), (3, ch, ch), (1, ch), (ch, ch), (1, ch)]
    like = lambda a: jax.ShapeDtypeStruct(a.shape, a.dtype)
    return pl.pallas_call(
        hand_over,
        name="hand_over",
        in_specs=[vmem] * 3,
        out_specs=[hbm] * 8,
        out_shape=[like(out), like(clips)] + [jax.ShapeDtypeStruct(s, F32) for s in shapes],
        scratch_shapes=[pltpu.VMEM(s, F32) for s in shapes]
        + [pltpu.SemaphoreType.DMA((out.shape[0], 2)), pltpu.SemaphoreType.DMA((6,))],
        compiler_params=pltpu.CompilerParams(vmem_limit_bytes=8 << 20),
    )


def body(rows, parts, clips_in, cw, cb, dw, db, mw, mb, counts, groups, out_grad):
    clips, ch, span = out_grad.shape
    pieces = -(-(4 * ch + 16) // PIECE)
    layer_out, clips_grad, sums = layer_call(rows, parts, clips, span, pieces)(
        counts, groups, clips_in, out_grad, cw.transpose(0, 2, 1), dw.transpose(2, 0, 1), mw, cb[None], db[None], mb[None]
    )
    layer_out, clips_grad, cg, cbg, dg, dbg, mg, mbg = hand_over_call(layer_out, clips_grad)(
        layer_out, clips_grad, sums.reshape(pieces * PIECE, 2 * ch)
    )
    return (layer_out, clips_grad, cg.transpose(0, 2, 1), cbg[0], dg.transpose(1, 2, 0), dbg[0], mg, mbg[0])


def solution(mesh):
    split = P("batch", None, "tm")
    placed = (split, P(), P(), P(), P(), P(), P(), P("batch"), P("batch"), split)
    return jax.shard_map(
        functools.partial(body, mesh.shape["batch"], mesh.shape["tm"]),
        mesh=mesh,
        in_specs=placed,
        out_specs=(split, split) + (P(),) * 6,
        check_vma=False,
    )
```

```python
import functools

import jax
import jax.numpy as jnp
from jax import lax
from jax.experimental import pallas as pl
from jax.experimental.pallas import tpu as pltpu
from jax.sharding import PartitionSpec as P

DILATION = 27
EDGE = 128
OFF = 2 * EDGE
CHUNK = 4096
SUB = 256
SUMS = 1024
RATIO = 2
ROWS = 16
OWNERS = 8
MESH = pl.DeviceIdType.MESH
F32 = jnp.float32
BF16 = jnp.bfloat16
C0 = 0.7978845608028654
C1 = 0.044715


def dot(a, b):
    return lax.dot_general(a, b, (((1,), (0,)), ((), ())), preferred_element_type=F32)


def dot_t(a, b):
    return lax.dot_general(a, b, (((1,), (1,)), ((), ())), preferred_element_type=F32)


def stack(*rows):
    return jnp.concatenate(rows, axis=0)


def beside(*parts):
    return jnp.concatenate(parts, axis=1)


def gelu_parts(half):
    square = half * half
    t = jnp.tanh(half * (2 * C0 + (8 * C0 * C1) * square))
    up = 1.0 + t
    value = half * up
    return value, up + (value * (1.0 - t)) * (2 * C0 + (24 * C0 * C1) * square)


def tall(rows, copies):
    return jnp.concatenate([rows] * copies, axis=0)


def wide(tile, count):
    return jnp.concatenate([tile] * count, axis=1)


def lane_groups(value):
    total = value[:, :EDGE]
    for start in range(EDGE, value.shape[1], EDGE):
        total = total + value[:, start : start + EDGE]
    return total


def owner_list(rows, parts, blocks):
    half = parts // 2
    order = sorted(range(half), key=lambda q: abs(2 * q - half + 1))
    spots = [r * parts + 2 * q + 1 for q in order for r in range(rows)][:OWNERS]
    share = blocks // len(spots)
    return [
        (home, k * share, share if k + 1 < len(spots) else blocks - k * share) for k, home in enumerate(spots)
    ]


def layer(
    rows,
    parts,
    owners,
    counts_ref,
    groups_ref,
    x_ref,
    og_ref,
    cw_ref,
    dw_ref,
    mw_ref,
    cb_ref,
    db_ref,
    mb_ref,
    outs,
    dxs,
    total_ref,
    wc,
    wd,
    wm,
    wdt,
    wct,
    biases,
    x0,
    x1,
    bg,
    x0p,
    x1m,
    half,
    slope,
    mid,
    midm,
    midp,
    gated,
    pre,
    prem,
    prep,
    grad,
    gradm,
    gradp,
    xh,
    ogh,
    pconv,
    pdil,
    pmix,
    psum,
    mask_high,
    mask_low,
    parcel,
    slots,
    counts,
    groups,
    cw,
    dw,
    mw,
    cb,
    db,
    mb,
    small_sem,
    in_sem,
    send,
    recv,
    send1,
    recv1,
    send2,
    recv2,
):
    ch = 64
    clips, _, span = og_ref.shape
    chunk = min(CHUNK, span)
    count = rows * parts
    row, place = lax.axis_index("batch"), lax.axis_index("tm")
    me = row * parts + place
    base = place * span

    def others(action):
        def step(r, carry):
            target = lax.rem(me + r, count)
            action(target // parts, lax.rem(target, parts))
            return carry

        lax.fori_loop(1, count, step, 0)

    inside = pl.ds(OFF, span)

    def fetches(b):
        return [
            pltpu.make_async_copy(x_ref.at[b, pl.ds(0, ch)], x0.at[b, :, inside], in_sem.at[b, 0]),
            pltpu.make_async_copy(x_ref.at[b, pl.ds(ch, ch)], x1.at[b, :, inside], in_sem.at[b, 1]),
            pltpu.make_async_copy(og_ref.at[b], bg.at[b, :, inside], in_sem.at[b, 2]),
        ]

    small = [
        pltpu.make_async_copy(src, dst, small_sem.at[k])
        for k, (src, dst) in enumerate(
            (
                (cw_ref, cw),
                (dw_ref, dw),
                (mw_ref, mw),
                (cb_ref, cb),
                (db_ref, db),
                (mb_ref, mb),
                (counts_ref, counts),
                (groups_ref, groups),
            )
        )
    ]
    for fetch in fetches(0)[:2] + small + fetches(0)[2:]:
        fetch.start()
    xh[...] = jnp.zeros(xh.shape, BF16)
    ogh[...] = jnp.zeros(ogh.shape, BF16)
    barrier = pltpu.get_barrier_semaphore()
    others(lambda r, p: pl.semaphore_signal(barrier, inc=1, device_id=(r, p), device_id_type=MESH))

    for fetch in small:
        fetch.wait()
    flip = lambda w: w.astype(F32).T.astype(BF16)
    taps = [cw[:, k, :] for k in range(4)]
    zero = jnp.zeros((ch, ch), BF16)
    for k in range(4):
        wc[:, k * ch : (k + 1) * ch] = taps[k] * 0.5
    for k in range(3):
        wd[:ch, k * ch : (k + 1) * ch] = dw[k] * 0.5
        wd[ch:, k * ch : (k + 1) * ch] = zero
        wdt[:, k * ch : (k + 1) * ch] = flip(dw[k]) * 0.5
    wm[...] = mw[...] * 0.5
    wd[:ch, 3 * ch :] = zero
    wd[ch:, 3 * ch :] = flip(mw[...]) * 0.5
    back = [flip(tap) for tap in taps]
    wct[:ch, :] = beside(back[3], back[1], zero)
    wct[ch:, :] = beside(zero, back[2], back[0])
    for k, line in enumerate((cb, db, mb)):
        biases[k] = jnp.broadcast_to(line[...] * 0.5, (EDGE, ch)).T

    lanes = span + 4 * EDGE
    frame = base - OFF + lax.broadcasted_iota(jnp.int32, (16, lanes), 1)
    for b in range(clips):
        valid = jnp.minimum(lax.shift_right_logical(counts[b], groups[b]), span * parts)
        mask = jnp.where((frame >= 0) & (frame < valid), 1.0, 0.0)
        mask_high[b] = mask[:8]
        mask_low[b] = mask.astype(BF16)

    for ref, at in ((gradm, OFF), (gradm, OFF + span), (grad, OFF + span)):
        ref[:, :, at : at + EDGE] = jnp.zeros((clips, ch, EDGE), BF16)
    for ref in (pconv, pdil, pmix, psum):
        ref[...] = jnp.zeros(ref.shape, F32)

    def masks(b, t, n):
        return mask_high[b, :, t + OFF : t + OFF + n]

    def low_masks(b, t, n):
        return mask_low[b, :, t + OFF : t + OFF + n]

    def put(ref, b, start, value):
        ref[b, :, start : start + value.shape[1]] = value

    has = (place > 0, place < parts - 1)
    other = (place - 1, place + 1)

    def moves(side):
        cut = pl.ds(0, EDGE) if side == 0 else pl.ds(span - EDGE, EDGE)
        return [
            pltpu.make_async_remote_copy(
                src_ref=src.at[:, :, cut],
                dst_ref=dst.at[1 - side],
                send_sem=send.at[side, k],
                recv_sem=recv.at[1 - side, k],
                device_id=(row, other[side]),
                device_id_type=MESH,
            )
            for k, (src, dst) in enumerate(((x_ref, xh), (og_ref, ogh)))
        ]

    def spot(t, n):
        return slice(t + OFF, t + OFF + n)

    def gather(ref, where):
        return beside(*[ref[b, :, spot(t, n)] for b, t, n in where])

    def cuts(where):
        at = 0
        for b, t, n in where:
            yield b, t, n, slice(at, at + n)
            at += n

    def spread(refs, where, step, low):
        now, before, after = refs
        for b, t, n, cut in cuts(where):
            now[b, :, spot(t, n)] = low[:, cut]
            put(before, b, t + OFF + step, low[:, cut])
            put(after, b, t + OFF - step, low[:, cut])

    def lows(where):
        return beside(*[tall(low_masks(b, t, n), ch // 16) for b, t, n in where])

    def stage0(b, t, n):
        here = spot(t, n)
        low = lows([(b, t, n)])
        even = x0[b, :, here] * low
        x0[b, :, here] = even
        put(x0p, b, t + OFF - 1, even)
        put(x1m, b, t + OFF + 1, x1[b, :, here])

    def tiles(where):
        found = []
        for b, t, n, cut in cuts(where):
            at = t
            while at < t + n:
                stop = min([at + SUB, t + n] + [border for border in (0, span) if border > at])
                found.append(((b, at, stop - at), slice(cut.start + at - t, cut.start + stop - t)))
                at = stop
        return found

    def stage1(where):
        taps = stack(gather(x1m, where), gather(x0, where), gather(x1, where), gather(x0p, where))
        product = dot(wc[...], taps)
        yield
        for (b, t, n), cut in tiles(where):
            h = product[:, cut] + wide(biases[0], n // EDGE)
            value, s = gelu_parts(h)
            half[b, :, spot(t, n)] = h
            slope[b, :, spot(t, n)] = s
            spread((mid, midm, midp), [(b, t, n)], DILATION, value.astype(BF16) * lows([(b, t, n)]))
            yield

    def own(where):
        kept = [(b, max(t, 0), min(t + n, span) - max(t, 0)) for b, t, n in where]
        return kept, [
            slice(cut.start + kt - t, cut.start + kt - t + kn)
            for (b, t, n, cut), (_, kt, kn) in zip(cuts(where), kept)
        ]

    def inside_of(t, n):
        return 0 <= t and t + n <= span

    def stage2(where):
        taps = stack(gather(midm, where), gather(mid, where), gather(midp, where), gather(bg, where))
        both = dot(wd[...], taps)
        yield
        lows_of, kept = [], []
        for (b, t, n), cut in tiles(where):
            d = both[:ch, cut] + wide(biases[1], n // EDGE)
            value, s = gelu_parts(d)
            pg = both[ch:, cut] * s
            spread((pre, prem, prep), [(b, t, n)], DILATION, pg.astype(BF16))
            if inside_of(t, n):
                low = value.astype(BF16)
                gated[b, :, t : t + n] = low
                psum[1] += lane_groups(pg)
                lows_of.append(low)
                kept.append((b, t, n))
            yield
        low = beside(*lows_of)
        pmix[:, : ch + 16] += dot_t(gather(bg, kept), stack(low, jnp.ones((16, low.shape[1]), BF16)))
        yield

    def stage3(where, halo=None):
        mid_grad = dot(wdt[...], stack(gather(prep, where), gather(pre, where), gather(prem, where)))
        yield
        for (b, t, n), cut in tiles(where):
            mask = tall(masks(b, t, n), ch // 8)
            here = spot(t, n)
            g = (bg[b, :, here].astype(F32) + mid_grad[:, cut] * slope[b, :, here]) * mask
            low = g.astype(BF16)
            if inside_of(t, n):
                psum[0] += lane_groups(g)
                grad[b, :, spot(t, n)] = low
                put(gradm, b, t + OFF + 1, low)
            elif halo is not None:
                halo.append((b, t, low))
            yield

    def by_steps(sums, where):
        for b, t, n in where:
            for k in range(0, n, SUMS):
                sums([(b, t + k, min(SUMS, n - k))])
                yield

    def dilated_sums(where):
        pdil[...] += dot_t(
            stack(gather(pre, where), gather(prem, where)), stack(gather(mid, where), gather(midm, where))
        )

    def strided_sums(where):
        pconv[...] += dot_t(
            stack(gather(grad, where), gather(gradm, where)), stack(gather(x1m, where), gather(x0, where))
        )

    def pieces_of(b, margin):
        edges = [margin] + list(range(chunk, span - margin, chunk)) + [span - margin]
        return [(b, t, e - t) for t, e in zip(edges, edges[1:])]

    def first(b):
        for t in range(0, span, chunk):
            stage0(b, t, chunk)
            yield
        for piece in pieces_of(b, EDGE):
            yield from stage1([piece])

    def later(piece):
        b, t, n = piece
        skip = EDGE if t == 3 * EDGE else 0
        return b, t + skip, n - skip

    def second(b):
        for t in range(0, span, chunk):
            bg[b, :, spot(t, chunk)] = bg[b, :, spot(t, chunk)] * lows([(b, t, chunk)])
            yield
        for piece in pieces_of(b, 2 * EDGE):
            yield from stage2([piece])
        for piece in pieces_of(b, 3 * EDGE):
            yield from stage3([piece])
            yield from by_steps(dilated_sums, [piece])
            yield from by_steps(strided_sums, [later(piece)])

    def mix(main, side, ratio):
        done = object()
        while True:
            ended = [next(main, done) is done for _ in range(ratio)]
            if next(side, done) is done and ended[-1]:
                return

    def run(work):
        for _ in work:
            pass

    def edge(width):
        return [
            (b, -EDGE if side == 0 else span - width, width + EDGE) for b in range(clips) for side in range(2)
        ]

    def outside():
        for b, t, n in edge(0):
            side = 0 if t < 0 else 1
            low = lows([(b, t, n)])
            even = xh[side, b, :ch] * low
            odd = xh[side, b, ch:]
            x0[b, :, spot(t, n)] = even
            x1[b, :, spot(t, n)] = odd
            put(x0p, b, t + OFF - 1, even)
            put(x1m, b, t + OFF + 1, odd)
            bg[b, :, spot(t, n)] = ogh[side, b] * low
        yield
        yield from stage1(edge(EDGE))
        yield from stage2(edge(2 * EDGE))
        halo = []
        yield from stage3(edge(3 * EDGE), halo)
        dilated_sums(own(edge(3 * EDGE))[0])
        strided_sums([(b, max(t, 0), 4 * EDGE) for b, t, _ in edge(3 * EDGE)])
        for b, t, low in halo:
            if t < 0:
                put(gradm, b, t + OFF + 1, low)
            else:
                grad[b, :, spot(t, EDGE)] = low
        yield

    def arrive(b):
        for fetch in fetches(b):
            fetch.wait()

    for fetch in fetches(0)[:2]:
        fetch.wait()
    for fetch in fetches(1):
        fetch.start()
    run(first(0))
    fetches(0)[2].wait()
    for b in range(clips - 1):
        arrive(b + 1)
        if b + 2 < clips:
            for fetch in fetches(b + 2):
                fetch.start()
        mix(second(b), first(b + 1), RATIO)
        if b == 0:
            pl.semaphore_wait(barrier, count - 1)
            for side in range(2):
                @pl.when(has[side])
                def _():
                    for move in moves(side):
                        move.start()

    for side in range(2):
        @pl.when(has[side])
        def _():
            for move in moves(1 - side):
                move.wait_recv()
    mix(second(clips - 1), outside(), RATIO)

    flat = [pconv[...], pdil[:ch, :], beside(pdil[ch:, :ch], pmix[:, :ch])]
    lines = [jnp.sum(psum[k].T, axis=0, keepdims=True) for k in range(2)]
    lines.append(pmix[:, ch:].T[:1, :])
    lines = stack(*lines, jnp.zeros((ROWS - 3, ch), F32))
    flat.append(beside(lines, jnp.zeros_like(lines)))
    at = 0
    for block in flat:
        for start in range(0, block.shape[0], ROWS):
            parcel[at] = block[start : start + ROWS, :].astype(BF16)
            at += 1
    for home, start, n in owners:
        @pl.when(me != home)
        def _():
            pltpu.make_async_remote_copy(
                src_ref=parcel.at[pl.ds(start, n)],
                dst_ref=slots.at[lax.rem(me - home + count, count) - 1, pl.ds(0, n)],
                send_sem=send1,
                recv_sem=recv1,
                device_id=(home // parts, home % parts),
                device_id_type=MESH,
            ).start()

    def third(b, carry):
        for t in range(0, span, chunk):
            here = slice(t + OFF, t + OFF + chunk)
            there = slice(t, t + chunk)
            low = low_masks(b, t, chunk)
            total = half[b, :, here] + dot(wm[...], gated[b, :, there]) + wide(biases[2], chunk // EDGE)
            outs[b, :, there] = total.astype(BF16) * tall(low + low, ch // 16)
            put(gradp, b, t + OFF - 1, grad[b, :, slice(t + OFF, t + OFF + chunk + EDGE)])
            dx = dot(wct[...], stack(gradm[b, :, here], grad[b, :, here], gradp[b, :, here]))
            dxs[b, :, there] = dx.astype(BF16) * tall(low, 2 * ch // 16)
        return carry

    lax.fori_loop(0, clips, third, 0)

    sizes = sorted({n for _, _, n in owners})
    blocks = parcel.shape[0]
    groups_of = [
        (n, [(home, start) for home, start, m in owners if m == n]) for n in sizes
    ]

    def is_one(homes):
        return functools.reduce(jnp.logical_or, [me == home for home, _ in homes])

    for n, homes in groups_of:
        @pl.when(is_one(homes))
        def _():
            start = sum(jnp.where(me == home, first_block, 0) for home, first_block in homes)
            mine = pl.ds(start, n)
            came = slots.at[:, pl.ds(0, n)]
            pltpu.make_async_copy(came, came, recv1).wait()
            total = parcel[mine].astype(F32)
            for k in range(count - 1):
                total = total + slots[k, :n].astype(F32)
            total_ref[mine] = total.astype(BF16)
            for k in range(1, count):
                target = lax.rem(me + k, count)
                pltpu.make_async_remote_copy(
                    src_ref=total_ref.at[mine],
                    dst_ref=total_ref.at[mine],
                    send_sem=send2,
                    recv_sem=recv2,
                    device_id=(target // parts, lax.rem(target, parts)),
                    device_id_type=MESH,
                ).start()

    for side in range(2):
        @pl.when(has[side])
        def _():
            for move in moves(side):
                move.wait_send()
    owner = is_one([(home, start) for home, start, _ in owners])
    for n, homes in groups_of:
        @pl.when(is_one(homes))
        def _():
            rest = total_ref.at[pl.ds(0, blocks - n)]
            pltpu.make_async_copy(rest, rest, recv2).wait()
            for _ in range(1, count):
                one = total_ref.at[pl.ds(0, n)]
                pltpu.make_async_copy(one, one, send2).wait()
            sent = parcel.at[pl.ds(0, blocks - n)]
            pltpu.make_async_copy(sent, sent, send1).wait()

    @pl.when(jnp.logical_not(owner))
    def _():
        pltpu.make_async_copy(total_ref, total_ref, recv2).wait()
        pltpu.make_async_copy(parcel, parcel, send1).wait()


def layer_call(rows, parts, clips, span, blocks):
    ch = 64
    lanes = span + 4 * EDGE
    vmem = pl.BlockSpec(memory_space=pltpu.VMEM)
    hbm = pl.BlockSpec(memory_space=pl.ANY)
    low = pltpu.VMEM((clips, ch, lanes), BF16)
    high = pltpu.VMEM((clips, ch, lanes), F32)
    dma = pltpu.SemaphoreType.DMA
    widest = max(n for _, _, n in owner_list(rows, parts, blocks))
    return pl.pallas_call(
        functools.partial(layer, rows, parts, owner_list(rows, parts, blocks)),
        name="layer",
        in_specs=[hbm] * 10,
        out_specs=[vmem, vmem, vmem],
        out_shape=[
            pltpu.VMEM((clips, ch, span), BF16),
            pltpu.VMEM((clips, 2 * ch, span), BF16),
            pltpu.VMEM((blocks, ROWS, 2 * ch), BF16),
        ],
        scratch_shapes=[
            pltpu.VMEM((ch, 4 * ch), BF16),
            pltpu.VMEM((2 * ch, 4 * ch), BF16),
            pltpu.VMEM((ch, ch), BF16),
            pltpu.VMEM((ch, 3 * ch), BF16),
            pltpu.VMEM((2 * ch, 3 * ch), BF16),
            pltpu.VMEM((3, ch, EDGE), F32),
        ]
        + [low] * 5
        + [high] * 2
        + [low] * 3
        + [pltpu.VMEM((clips, ch, span), BF16)]
        + [low] * 6
        + [
            pltpu.VMEM((2, clips, 2 * ch, EDGE), BF16),
            pltpu.VMEM((2, clips, ch, EDGE), BF16),
            pltpu.VMEM((2 * ch, 2 * ch), F32),
            pltpu.VMEM((2 * ch, 2 * ch), F32),
            pltpu.VMEM((ch, 2 * ch), F32),
            pltpu.VMEM((2, ch, EDGE), F32),
            pltpu.VMEM((clips, 8, lanes), F32),
            pltpu.VMEM((clips, 16, lanes), BF16),
            pltpu.VMEM((blocks, ROWS, 2 * ch), BF16),
            pltpu.VMEM((rows * parts - 1, widest, ROWS, 2 * ch), BF16),
            pltpu.SMEM((clips,), jnp.int32),
            pltpu.SMEM((clips,), jnp.int32),
            pltpu.VMEM((ch, 4, ch), BF16),
            pltpu.VMEM((3, ch, ch), BF16),
            pltpu.VMEM((ch, ch), BF16),
            pltpu.VMEM((1, ch), F32),
            pltpu.VMEM((1, ch), F32),
            pltpu.VMEM((1, ch), F32),
            dma((8,)),
            dma((clips, 3)),
            dma((2, 2)),
            dma((2, 2)),
            dma,
            dma,
            dma,
            dma,
        ],
        compiler_params=pltpu.CompilerParams(collective_id=0, has_side_effects=True, vmem_limit_bytes=54 << 20),
    )


def hand_over(out_in, clips_in, sums, *refs):
    out, clips = refs[:2]
    finals, (cg, cb, dg, db, mg, mb), (sem, small_sem) = refs[2:8], refs[8:14], refs[14:]
    ch = 64
    moves = []
    for b in range(out.shape[0]):
        for k, (src, dst) in enumerate(((out_in, out), (clips_in, clips))):
            moves.append(pltpu.make_async_copy(src.at[b], dst.at[b], sem.at[b, k]))
    for move in moves:
        move.start()
    at = lambda start, count: sums[start : start + count, :].astype(F32)
    low, high = at(0, ch), at(ch, ch)
    for k, block in enumerate((low[:, :ch], low[:, ch:], high[:, :ch], high[:, ch:])):
        cg[:, k, :] = block
    block = at(2 * ch, ch)
    dg[1] = block[:, :ch]
    dg[0] = block[:, ch:]
    block = at(3 * ch, ch)
    dg[2] = block[:, :ch]
    mg[...] = block[:, ch:]
    lines = at(4 * ch, 16)[:, :ch]
    for k, ref in enumerate((cb, db, mb)):
        ref[...] = lines[k : k + 1]
    for k, (src, dst) in enumerate(zip((cg, cb, dg, db, mg, mb), finals)):
        moves.append(pltpu.make_async_copy(src, dst, small_sem.at[k]))
        moves[-1].start()
    for move in moves:
        move.wait()


def hand_over_call(out, clips):
    ch = 64
    vmem = pl.BlockSpec(memory_space=pltpu.VMEM)
    hbm = pl.BlockSpec(memory_space=pl.ANY)
    shapes = [(ch, 4, ch), (1, ch), (3, ch, ch), (1, ch), (ch, ch), (1, ch)]
    like = lambda a: jax.ShapeDtypeStruct(a.shape, a.dtype)
    return pl.pallas_call(
        hand_over,
        name="hand_over",
        in_specs=[vmem] * 3,
        out_specs=[hbm] * 8,
        out_shape=[like(out), like(clips)] + [jax.ShapeDtypeStruct(s, F32) for s in shapes],
        scratch_shapes=[pltpu.VMEM(s, F32) for s in shapes]
        + [pltpu.SemaphoreType.DMA((out.shape[0], 2)), pltpu.SemaphoreType.DMA((6,))],
        compiler_params=pltpu.CompilerParams(vmem_limit_bytes=8 << 20),
    )


def body(rows, parts, clips_in, cw, cb, dw, db, mw, mb, counts, groups, out_grad):
    clips, ch, span = out_grad.shape
    blocks = (4 * ch + ROWS) // ROWS
    layer_out, clips_grad, sums = layer_call(rows, parts, clips, span, blocks)(
        counts, groups, clips_in, out_grad, cw.transpose(0, 2, 1), dw.transpose(2, 0, 1), mw, cb[None], db[None], mb[None]
    )
    layer_out, clips_grad, cg, cbg, dg, dbg, mg, mbg = hand_over_call(layer_out, clips_grad)(
        layer_out, clips_grad, sums.reshape(blocks * ROWS, 2 * ch)
    )
    return (layer_out, clips_grad, cg.transpose(0, 2, 1), cbg[0], dg.transpose(1, 2, 0), dbg[0], mg, mbg[0])


def solution(mesh):
    split = P("batch", None, "tm")
    placed = (split, P(), P(), P(), P(), P(), P(), P("batch"), P("batch"), split)
    return jax.shard_map(
        functools.partial(body, mesh.shape["batch"], mesh.shape["tm"]),
        mesh=mesh,
        in_specs=placed,
        out_specs=(split, split) + (P(),) * 6,
        check_vma=False,
    )
```

```python
import functools

import jax
import jax.numpy as jnp
from jax import lax
from jax.experimental import pallas as pl
from jax.experimental.pallas import tpu as pltpu
from jax.sharding import PartitionSpec as P

DILATION = 27
EDGE = 128
OFF = 2 * EDGE
CHUNK = 4096
SUB = 256
SUMS = 1024
RATIO = 2
ROWS = 16
OWNERS = 8
MESH = pl.DeviceIdType.MESH
F32 = jnp.float32
BF16 = jnp.bfloat16
C0 = 0.7978845608028654
C1 = 0.044715


def dot(a, b):
    return lax.dot_general(a, b, (((1,), (0,)), ((), ())), preferred_element_type=F32)


def dot_t(a, b):
    return lax.dot_general(a, b, (((1,), (1,)), ((), ())), preferred_element_type=F32)


def stack(*rows):
    return jnp.concatenate(rows, axis=0)


def beside(*parts):
    return jnp.concatenate(parts, axis=1)


def gelu_parts(half):
    square = half * half
    t = jnp.tanh(half * (2 * C0 + (8 * C0 * C1) * square))
    up = 1.0 + t
    value = half * up
    return value, up + (value * (1.0 - t)) * (2 * C0 + (24 * C0 * C1) * square)


def tall(rows, copies):
    return jnp.concatenate([rows] * copies, axis=0)


def wide(tile, count):
    return jnp.concatenate([tile] * count, axis=1)


def lane_groups(value):
    total = value[:, :EDGE]
    for start in range(EDGE, value.shape[1], EDGE):
        total = total + value[:, start : start + EDGE]
    return total


def owner_list(rows, parts, blocks):
    half = parts // 2
    order = sorted(range(half), key=lambda q: abs(2 * q - half + 1))
    spots = [r * parts + 2 * q + 1 for q in order for r in range(rows)][:OWNERS]
    share = blocks // len(spots)
    return [
        (home, k * share, share if k + 1 < len(spots) else blocks - k * share) for k, home in enumerate(spots)
    ]


def layer(
    rows,
    parts,
    owners,
    counts_ref,
    groups_ref,
    x_ref,
    og_ref,
    cw_ref,
    dw_ref,
    mw_ref,
    cb_ref,
    db_ref,
    mb_ref,
    outs,
    dxs,
    total_ref,
    wc,
    wd,
    wm,
    wdt,
    wct,
    biases,
    x0,
    x1,
    bg,
    x0p,
    x1m,
    half,
    slope,
    mid,
    midm,
    midp,
    gated,
    pre,
    prem,
    prep,
    grad,
    gradm,
    gradp,
    xh,
    ogh,
    pconv,
    pdil,
    pmix,
    psum,
    mask_high,
    mask_low,
    parcel,
    slots,
    counts,
    groups,
    cw,
    dw,
    mw,
    cb,
    db,
    mb,
    small_sem,
    in_sem,
    send,
    recv,
    send1,
    recv1,
    send2,
    recv2,
):
    ch = 64
    clips, _, span = og_ref.shape
    chunk = min(CHUNK, span)
    count = rows * parts
    row, place = lax.axis_index("batch"), lax.axis_index("tm")
    me = row * parts + place
    base = place * span

    def others(action):
        def step(r, carry):
            target = lax.rem(me + r, count)
            action(target // parts, lax.rem(target, parts))
            return carry

        lax.fori_loop(1, count, step, 0)

    inside = pl.ds(OFF, span)

    def fetches(b):
        return [
            pltpu.make_async_copy(x_ref.at[b, pl.ds(0, ch)], x0.at[b, :, inside], in_sem.at[b, 0]),
            pltpu.make_async_copy(x_ref.at[b, pl.ds(ch, ch)], x1.at[b, :, inside], in_sem.at[b, 1]),
            pltpu.make_async_copy(og_ref.at[b], bg.at[b, :, inside], in_sem.at[b, 2]),
        ]

    small = [
        pltpu.make_async_copy(src, dst, small_sem.at[k])
        for k, (src, dst) in enumerate(
            (
                (cw_ref, cw),
                (dw_ref, dw),
                (mw_ref, mw),
                (cb_ref, cb),
                (db_ref, db),
                (mb_ref, mb),
                (counts_ref, counts),
                (groups_ref, groups),
            )
        )
    ]
    for fetch in fetches(0)[:2] + small + fetches(0)[2:]:
        fetch.start()
    xh[...] = jnp.zeros(xh.shape, BF16)
    ogh[...] = jnp.zeros(ogh.shape, BF16)
    barrier = pltpu.get_barrier_semaphore()
    others(lambda r, p: pl.semaphore_signal(barrier, inc=1, device_id=(r, p), device_id_type=MESH))

    for fetch in small:
        fetch.wait()
    flip = lambda w: w.astype(F32).T.astype(BF16)
    taps = [cw[:, k, :] for k in range(4)]
    zero = jnp.zeros((ch, ch), BF16)
    for k in range(4):
        wc[:, k * ch : (k + 1) * ch] = taps[k] * 0.5
    for k in range(3):
        wd[:ch, k * ch : (k + 1) * ch] = dw[k] * 0.5
        wd[ch:, k * ch : (k + 1) * ch] = zero
        wdt[:, k * ch : (k + 1) * ch] = flip(dw[k]) * 0.5
    wm[...] = mw[...] * 0.5
    wd[:ch, 3 * ch :] = zero
    wd[ch:, 3 * ch :] = flip(mw[...]) * 0.5
    back = [flip(tap) for tap in taps]
    wct[:ch, :] = beside(back[3], back[1], zero)
    wct[ch:, :] = beside(zero, back[2], back[0])
    for k, line in enumerate((cb, db, mb)):
        biases[k] = jnp.broadcast_to(line[...] * 0.5, (EDGE, ch)).T

    lanes = span + 4 * EDGE
    frame = base - OFF + lax.broadcasted_iota(jnp.int32, (16, lanes), 1)
    for b in range(clips):
        valid = jnp.minimum(lax.shift_right_logical(counts[b], groups[b]), span * parts)
        mask = jnp.where((frame >= 0) & (frame < valid), 1.0, 0.0)
        mask_high[b] = mask[:8]
        mask_low[b] = mask.astype(BF16)

    for ref, at in ((gradm, OFF), (gradm, OFF + span), (grad, OFF + span)):
        ref[:, :, at : at + EDGE] = jnp.zeros((clips, ch, EDGE), BF16)
    for ref in (pconv, pdil, pmix, psum):
        ref[...] = jnp.zeros(ref.shape, F32)

    def masks(b, t, n):
        return mask_high[b, :, t + OFF : t + OFF + n]

    def low_masks(b, t, n):
        return mask_low[b, :, t + OFF : t + OFF + n]

    def put(ref, b, start, value):
        ref[b, :, start : start + value.shape[1]] = value

    has = (place > 0, place < parts - 1)
    other = (place - 1, place + 1)

    def moves(side):
        cut = pl.ds(0, EDGE) if side == 0 else pl.ds(span - EDGE, EDGE)
        return [
            pltpu.make_async_remote_copy(
                src_ref=src.at[:, :, cut],
                dst_ref=dst.at[1 - side],
                send_sem=send.at[side, k],
                recv_sem=recv.at[1 - side, k],
                device_id=(row, other[side]),
                device_id_type=MESH,
            )
            for k, (src, dst) in enumerate(((x_ref, xh), (og_ref, ogh)))
        ]

    def spot(t, n):
        return slice(t + OFF, t + OFF + n)

    def gather(ref, where):
        return beside(*[ref[b, :, spot(t, n)] for b, t, n in where])

    def cuts(where):
        at = 0
        for b, t, n in where:
            yield b, t, n, slice(at, at + n)
            at += n

    def spread(refs, where, step, low):
        now, before, after = refs
        for b, t, n, cut in cuts(where):
            now[b, :, spot(t, n)] = low[:, cut]
            put(before, b, t + OFF + step, low[:, cut])
            put(after, b, t + OFF - step, low[:, cut])

    def lows(where):
        return beside(*[tall(low_masks(b, t, n), ch // 16) for b, t, n in where])

    def stage0(b, t, n):
        here = spot(t, n)
        low = lows([(b, t, n)])
        even = x0[b, :, here] * low
        x0[b, :, here] = even
        put(x0p, b, t + OFF - 1, even)
        put(x1m, b, t + OFF + 1, x1[b, :, here])

    def tiles(where):
        found = []
        for b, t, n, cut in cuts(where):
            at = t
            while at < t + n:
                stop = min([at + SUB, t + n] + [border for border in (0, span) if border > at])
                found.append(((b, at, stop - at), slice(cut.start + at - t, cut.start + stop - t)))
                at = stop
        return found

    def stage1(where):
        taps = stack(gather(x1m, where), gather(x0, where), gather(x1, where), gather(x0p, where))
        product = dot(wc[...], taps)
        yield
        for (b, t, n), cut in tiles(where):
            h = product[:, cut] + wide(biases[0], n // EDGE)
            value, s = gelu_parts(h)
            half[b, :, spot(t, n)] = h
            slope[b, :, spot(t, n)] = s
            spread((mid, midm, midp), [(b, t, n)], DILATION, value.astype(BF16) * lows([(b, t, n)]))
            yield

    def own(where):
        kept = [(b, max(t, 0), min(t + n, span) - max(t, 0)) for b, t, n in where]
        return kept, [
            slice(cut.start + kt - t, cut.start + kt - t + kn)
            for (b, t, n, cut), (_, kt, kn) in zip(cuts(where), kept)
        ]

    def inside_of(t, n):
        return 0 <= t and t + n <= span

    def stage2(where):
        taps = stack(gather(midm, where), gather(mid, where), gather(midp, where), gather(bg, where))
        both = dot(wd[...], taps)
        yield
        lows_of, kept = [], []
        for (b, t, n), cut in tiles(where):
            d = both[:ch, cut] + wide(biases[1], n // EDGE)
            value, s = gelu_parts(d)
            pg = both[ch:, cut] * s
            spread((pre, prem, prep), [(b, t, n)], DILATION, pg.astype(BF16))
            if inside_of(t, n):
                low = value.astype(BF16)
                gated[b, :, t : t + n] = low
                psum[1] += lane_groups(pg)
                lows_of.append(low)
                kept.append((b, t, n))
            yield
        low = beside(*lows_of)
        pmix[:, : ch + 16] += dot_t(gather(bg, kept), stack(low, jnp.ones((16, low.shape[1]), BF16)))
        yield

    def stage3(where, halo=None):
        mid_grad = dot(wdt[...], stack(gather(prep, where), gather(pre, where), gather(prem, where)))
        yield
        for (b, t, n), cut in tiles(where):
            mask = tall(masks(b, t, n), ch // 8)
            here = spot(t, n)
            g = (bg[b, :, here].astype(F32) + mid_grad[:, cut] * slope[b, :, here]) * mask
            low = g.astype(BF16)
            if inside_of(t, n):
                psum[0] += lane_groups(g)
                grad[b, :, spot(t, n)] = low
                put(gradm, b, t + OFF + 1, low)
            elif halo is not None:
                halo.append((b, t, low))
            yield

    def by_steps(sums, where):
        for b, t, n in where:
            for k in range(0, n, SUMS):
                sums([(b, t + k, min(SUMS, n - k))])
                yield

    def dilated_sums(where):
        pdil[...] += dot_t(
            stack(gather(pre, where), gather(prem, where)), stack(gather(mid, where), gather(midm, where))
        )

    def strided_sums(where):
        pconv[...] += dot_t(
            stack(gather(grad, where), gather(gradm, where)), stack(gather(x1m, where), gather(x0, where))
        )

    def pieces_of(b, margin):
        edges = [margin] + list(range(chunk, span - margin, chunk)) + [span - margin]
        return [(b, t, e - t) for t, e in zip(edges, edges[1:])]

    def first(b):
        for t in range(0, span, chunk):
            stage0(b, t, chunk)
            yield
        for piece in pieces_of(b, EDGE):
            yield from stage1([piece])

    def later(piece):
        b, t, n = piece
        skip = EDGE if t == 3 * EDGE else 0
        return b, t + skip, n - skip

    def second(b):
        for t in range(0, span, chunk):
            bg[b, :, spot(t, chunk)] = bg[b, :, spot(t, chunk)] * lows([(b, t, chunk)])
            yield
        for piece in pieces_of(b, 2 * EDGE):
            yield from stage2([piece])
        for piece in pieces_of(b, 3 * EDGE):
            yield from stage3([piece])
            yield from by_steps(dilated_sums, [piece])
            yield from by_steps(strided_sums, [later(piece)])

    def mix(main, side, ratio):
        done = object()
        while True:
            ended = [next(main, done) is done for _ in range(ratio)]
            if next(side, done) is done and ended[-1]:
                return

    def run(work):
        for _ in work:
            pass

    def edge(width):
        return [
            (b, -EDGE if side == 0 else span - width, width + EDGE) for b in range(clips) for side in range(2)
        ]

    def outside():
        for b, t, n in edge(0):
            side = 0 if t < 0 else 1
            low = lows([(b, t, n)])
            even = xh[side, b, :ch] * low
            odd = xh[side, b, ch:]
            x0[b, :, spot(t, n)] = even
            x1[b, :, spot(t, n)] = odd
            put(x0p, b, t + OFF - 1, even)
            put(x1m, b, t + OFF + 1, odd)
            bg[b, :, spot(t, n)] = ogh[side, b] * low
        yield
        yield from stage1(edge(EDGE))
        yield from stage2(edge(2 * EDGE))
        yield from stage3(own(edge(3 * EDGE))[0])
        dilated_sums(own(edge(3 * EDGE))[0])
        strided_sums([(b, max(t, 0), 4 * EDGE) for b, t, _ in edge(3 * EDGE)])
        yield

    def arrive(b):
        for fetch in fetches(b):
            fetch.wait()

    for fetch in fetches(0)[:2]:
        fetch.wait()
    for fetch in fetches(1):
        fetch.start()
    run(first(0))
    fetches(0)[2].wait()
    arrive(1)
    for b in range(2, clips):
        for fetch in fetches(b):
            fetch.start()
    mix(second(0), first(1), RATIO)
    pl.semaphore_wait(barrier, count - 1)
    for side in range(2):
        @pl.when(has[side])
        def _():
            for move in moves(side):
                move.start()
    for b in range(2, clips):
        arrive(b)
    for b in range(1, clips - 1):
        mix(second(b), first(b + 1), RATIO)

    for side in range(2):
        @pl.when(has[side])
        def _():
            for move in moves(1 - side):
                move.wait_recv()
    mix(second(clips - 1), outside(), RATIO)

    flat = [pconv[...], pdil[:ch, :], beside(pdil[ch:, :ch], pmix[:, :ch])]
    lines = [jnp.sum(psum[k].T, axis=0, keepdims=True) for k in range(2)]
    lines.append(pmix[:, ch:].T[:1, :])
    lines = stack(*lines, jnp.zeros((ROWS - 3, ch), F32))
    flat.append(beside(lines, jnp.zeros_like(lines)))
    at = 0
    for block in flat:
        for start in range(0, block.shape[0], ROWS):
            parcel[at] = block[start : start + ROWS, :].astype(BF16)
            at += 1
    for home, start, n in owners:
        @pl.when(me != home)
        def _():
            pltpu.make_async_remote_copy(
                src_ref=parcel.at[pl.ds(start, n)],
                dst_ref=slots.at[lax.rem(me - home + count, count) - 1, pl.ds(0, n)],
                send_sem=send1,
                recv_sem=recv1,
                device_id=(home // parts, home % parts),
                device_id_type=MESH,
            ).start()

    halo = []
    run(stage3([(b, t, EDGE) for b in range(clips) for t in (-EDGE, span)], halo))
    for b, t, low in halo:
        if t < 0:
            put(gradm, b, t + OFF + 1, low)
        else:
            grad[b, :, spot(t, EDGE)] = low

    def third(b, carry):
        for t in range(0, span, chunk):
            here = slice(t + OFF, t + OFF + chunk)
            there = slice(t, t + chunk)
            low = low_masks(b, t, chunk)
            total = half[b, :, here] + dot(wm[...], gated[b, :, there]) + wide(biases[2], chunk // EDGE)
            outs[b, :, there] = total.astype(BF16) * tall(low + low, ch // 16)
            put(gradp, b, t + OFF - 1, grad[b, :, slice(t + OFF, t + OFF + chunk + EDGE)])
            dx = dot(wct[...], stack(gradm[b, :, here], grad[b, :, here], gradp[b, :, here]))
            dxs[b, :, there] = dx.astype(BF16) * tall(low, 2 * ch // 16)
        return carry

    lax.fori_loop(0, clips, third, 0)

    sizes = sorted({n for _, _, n in owners})
    blocks = parcel.shape[0]
    groups_of = [
        (n, [(home, start) for home, start, m in owners if m == n]) for n in sizes
    ]

    def is_one(homes):
        return functools.reduce(jnp.logical_or, [me == home for home, _ in homes])

    for n, homes in groups_of:
        @pl.when(is_one(homes))
        def _():
            start = sum(jnp.where(me == home, first_block, 0) for home, first_block in homes)
            mine = pl.ds(start, n)
            came = slots.at[:, pl.ds(0, n)]
            pltpu.make_async_copy(came, came, recv1).wait()
            total = parcel[mine].astype(F32)
            for k in range(count - 1):
                total = total + slots[k, :n].astype(F32)
            total_ref[mine] = total.astype(BF16)
            for k in range(1, count):
                target = lax.rem(me + k, count)
                pltpu.make_async_remote_copy(
                    src_ref=total_ref.at[mine],
                    dst_ref=total_ref.at[mine],
                    send_sem=send2,
                    recv_sem=recv2,
                    device_id=(target // parts, lax.rem(target, parts)),
                    device_id_type=MESH,
                ).start()

    for side in range(2):
        @pl.when(has[side])
        def _():
            for move in moves(side):
                move.wait_send()
    owner = is_one([(home, start) for home, start, _ in owners])
    for n, homes in groups_of:
        @pl.when(is_one(homes))
        def _():
            rest = total_ref.at[pl.ds(0, blocks - n)]
            pltpu.make_async_copy(rest, rest, recv2).wait()
            for _ in range(1, count):
                one = total_ref.at[pl.ds(0, n)]
                pltpu.make_async_copy(one, one, send2).wait()
            sent = parcel.at[pl.ds(0, blocks - n)]
            pltpu.make_async_copy(sent, sent, send1).wait()

    @pl.when(jnp.logical_not(owner))
    def _():
        pltpu.make_async_copy(total_ref, total_ref, recv2).wait()
        pltpu.make_async_copy(parcel, parcel, send1).wait()


def layer_call(rows, parts, clips, span, blocks):
    ch = 64
    lanes = span + 4 * EDGE
    vmem = pl.BlockSpec(memory_space=pltpu.VMEM)
    hbm = pl.BlockSpec(memory_space=pl.ANY)
    low = pltpu.VMEM((clips, ch, lanes), BF16)
    high = pltpu.VMEM((clips, ch, lanes), F32)
    dma = pltpu.SemaphoreType.DMA
    widest = max(n for _, _, n in owner_list(rows, parts, blocks))
    return pl.pallas_call(
        functools.partial(layer, rows, parts, owner_list(rows, parts, blocks)),
        name="layer",
        in_specs=[hbm] * 10,
        out_specs=[vmem, vmem, vmem],
        out_shape=[
            pltpu.VMEM((clips, ch, span), BF16),
            pltpu.VMEM((clips, 2 * ch, span), BF16),
            pltpu.VMEM((blocks, ROWS, 2 * ch), BF16),
        ],
        scratch_shapes=[
            pltpu.VMEM((ch, 4 * ch), BF16),
            pltpu.VMEM((2 * ch, 4 * ch), BF16),
            pltpu.VMEM((ch, ch), BF16),
            pltpu.VMEM((ch, 3 * ch), BF16),
            pltpu.VMEM((2 * ch, 3 * ch), BF16),
            pltpu.VMEM((3, ch, EDGE), F32),
        ]
        + [low] * 5
        + [high] * 2
        + [low] * 3
        + [pltpu.VMEM((clips, ch, span), BF16)]
        + [low] * 6
        + [
            pltpu.VMEM((2, clips, 2 * ch, EDGE), BF16),
            pltpu.VMEM((2, clips, ch, EDGE), BF16),
            pltpu.VMEM((2 * ch, 2 * ch), F32),
            pltpu.VMEM((2 * ch, 2 * ch), F32),
            pltpu.VMEM((ch, 2 * ch), F32),
            pltpu.VMEM((2, ch, EDGE), F32),
            pltpu.VMEM((clips, 8, lanes), F32),
            pltpu.VMEM((clips, 16, lanes), BF16),
            pltpu.VMEM((blocks, ROWS, 2 * ch), BF16),
            pltpu.VMEM((rows * parts - 1, widest, ROWS, 2 * ch), BF16),
            pltpu.SMEM((clips,), jnp.int32),
            pltpu.SMEM((clips,), jnp.int32),
            pltpu.VMEM((ch, 4, ch), BF16),
            pltpu.VMEM((3, ch, ch), BF16),
            pltpu.VMEM((ch, ch), BF16),
            pltpu.VMEM((1, ch), F32),
            pltpu.VMEM((1, ch), F32),
            pltpu.VMEM((1, ch), F32),
            dma((8,)),
            dma((clips, 3)),
            dma((2, 2)),
            dma((2, 2)),
            dma,
            dma,
            dma,
            dma,
        ],
        compiler_params=pltpu.CompilerParams(collective_id=0, has_side_effects=True, vmem_limit_bytes=54 << 20),
    )


def hand_over(out_in, clips_in, sums, *refs):
    out, clips = refs[:2]
    finals, (cg, cb, dg, db, mg, mb), (sem, small_sem) = refs[2:8], refs[8:14], refs[14:]
    ch = 64
    moves = []
    for b in range(out.shape[0]):
        for k, (src, dst) in enumerate(((out_in, out), (clips_in, clips))):
            moves.append(pltpu.make_async_copy(src.at[b], dst.at[b], sem.at[b, k]))
    for move in moves:
        move.start()
    at = lambda start, count: sums[start : start + count, :].astype(F32)
    low, high = at(0, ch), at(ch, ch)
    for k, block in enumerate((low[:, :ch], low[:, ch:], high[:, :ch], high[:, ch:])):
        cg[:, k, :] = block
    block = at(2 * ch, ch)
    dg[1] = block[:, :ch]
    dg[0] = block[:, ch:]
    block = at(3 * ch, ch)
    dg[2] = block[:, :ch]
    mg[...] = block[:, ch:]
    lines = at(4 * ch, 16)[:, :ch]
    for k, ref in enumerate((cb, db, mb)):
        ref[...] = lines[k : k + 1]
    for k, (src, dst) in enumerate(zip((cg, cb, dg, db, mg, mb), finals)):
        moves.append(pltpu.make_async_copy(src, dst, small_sem.at[k]))
        moves[-1].start()
    for move in moves:
        move.wait()


def hand_over_call(out, clips):
    ch = 64
    vmem = pl.BlockSpec(memory_space=pltpu.VMEM)
    hbm = pl.BlockSpec(memory_space=pl.ANY)
    shapes = [(ch, 4, ch), (1, ch), (3, ch, ch), (1, ch), (ch, ch), (1, ch)]
    like = lambda a: jax.ShapeDtypeStruct(a.shape, a.dtype)
    return pl.pallas_call(
        hand_over,
        name="hand_over",
        in_specs=[vmem] * 3,
        out_specs=[hbm] * 8,
        out_shape=[like(out), like(clips)] + [jax.ShapeDtypeStruct(s, F32) for s in shapes],
        scratch_shapes=[pltpu.VMEM(s, F32) for s in shapes]
        + [pltpu.SemaphoreType.DMA((out.shape[0], 2)), pltpu.SemaphoreType.DMA((6,))],
        compiler_params=pltpu.CompilerParams(vmem_limit_bytes=8 << 20),
    )


def body(rows, parts, clips_in, cw, cb, dw, db, mw, mb, counts, groups, out_grad):
    clips, ch, span = out_grad.shape
    blocks = (4 * ch + ROWS) // ROWS
    layer_out, clips_grad, sums = layer_call(rows, parts, clips, span, blocks)(
        counts, groups, clips_in, out_grad, cw.transpose(0, 2, 1), dw.transpose(2, 0, 1), mw, cb[None], db[None], mb[None]
    )
    layer_out, clips_grad, cg, cbg, dg, dbg, mg, mbg = hand_over_call(layer_out, clips_grad)(
        layer_out, clips_grad, sums.reshape(blocks * ROWS, 2 * ch)
    )
    return (layer_out, clips_grad, cg.transpose(0, 2, 1), cbg[0], dg.transpose(1, 2, 0), dbg[0], mg, mbg[0])


def solution(mesh):
    split = P("batch", None, "tm")
    placed = (split, P(), P(), P(), P(), P(), P(), P("batch"), P("batch"), split)
    return jax.shard_map(
        functools.partial(body, mesh.shape["batch"], mesh.shape["tm"]),
        mesh=mesh,
        in_specs=placed,
        out_specs=(split, split) + (P(),) * 6,
        check_vma=False,
    )
```

```python
import functools

import jax
import jax.numpy as jnp
from jax import lax
from jax.experimental import pallas as pl
from jax.experimental.pallas import tpu as pltpu
from jax.sharding import PartitionSpec as P

DILATION = 27
EDGE = 128
OFF = 2 * EDGE
CHUNK = 4096
SUB = 256
SUMS = 1024
RATIO = 2
ROWS = 16
OWNERS = 8
MESH = pl.DeviceIdType.MESH
F32 = jnp.float32
BF16 = jnp.bfloat16
C0 = 0.7978845608028654
C1 = 0.044715


def dot(a, b):
    return lax.dot_general(a, b, (((1,), (0,)), ((), ())), preferred_element_type=F32)


def dot_t(a, b):
    return lax.dot_general(a, b, (((1,), (1,)), ((), ())), preferred_element_type=F32)


def stack(*rows):
    return jnp.concatenate(rows, axis=0)


def beside(*parts):
    return jnp.concatenate(parts, axis=1)


def gelu_parts(half):
    square = half * half
    t = jnp.tanh(half * (2 * C0 + (8 * C0 * C1) * square))
    up = 1.0 + t
    value = half * up
    return value, up + (value * (1.0 - t)) * (2 * C0 + (24 * C0 * C1) * square)


def tall(rows, copies):
    return jnp.concatenate([rows] * copies, axis=0)


def wide(tile, count):
    return jnp.concatenate([tile] * count, axis=1)


def lane_groups(value):
    total = value[:, :EDGE]
    for start in range(EDGE, value.shape[1], EDGE):
        total = total + value[:, start : start + EDGE]
    return total


def owner_list(rows, parts, blocks):
    half = parts // 2
    order = sorted(range(half), key=lambda q: abs(2 * q - half + 1))
    spots = [r * parts + 2 * q + 1 for q in order for r in range(rows)][:OWNERS]
    share = blocks // len(spots)
    return [
        (home, k * share, share if k + 1 < len(spots) else blocks - k * share) for k, home in enumerate(spots)
    ]


def layer(
    rows,
    parts,
    owners,
    counts_ref,
    groups_ref,
    x_ref,
    og_ref,
    cw_ref,
    dw_ref,
    mw_ref,
    cb_ref,
    db_ref,
    mb_ref,
    outs,
    dxs,
    total_ref,
    wc,
    wd,
    wm,
    wdt,
    wct,
    biases,
    x0,
    x1,
    bg,
    x0p,
    x1m,
    half,
    slope,
    mid,
    midm,
    midp,
    gated,
    pre,
    prem,
    prep,
    grad,
    gradm,
    gradp,
    x_edge,
    og_edge,
    xh,
    ogh,
    pconv,
    pdil,
    pmix,
    psum,
    mask_high,
    mask_low,
    parcel,
    slots,
    counts,
    groups,
    cw,
    dw,
    mw,
    cb,
    db,
    mb,
    small_sem,
    in_sem,
    send,
    recv,
    send1,
    recv1,
    send2,
    recv2,
):
    ch = 64
    clips, _, span = og_ref.shape
    chunk = min(CHUNK, span)
    count = rows * parts
    row, place = lax.axis_index("batch"), lax.axis_index("tm")
    me = row * parts + place
    base = place * span

    def others(action):
        def step(r, carry):
            target = lax.rem(me + r, count)
            action(target // parts, lax.rem(target, parts))
            return carry

        lax.fori_loop(1, count, step, 0)

    inside = pl.ds(OFF, span)

    def fetches(b):
        return [
            pltpu.make_async_copy(x_ref.at[b, pl.ds(0, ch)], x0.at[b, :, inside], in_sem.at[b, 0]),
            pltpu.make_async_copy(x_ref.at[b, pl.ds(ch, ch)], x1.at[b, :, inside], in_sem.at[b, 1]),
            pltpu.make_async_copy(og_ref.at[b], bg.at[b, :, inside], in_sem.at[b, 2]),
        ]

    small = [
        pltpu.make_async_copy(src, dst, small_sem.at[k])
        for k, (src, dst) in enumerate(
            (
                (cw_ref, cw),
                (dw_ref, dw),
                (mw_ref, mw),
                (cb_ref, cb),
                (db_ref, db),
                (mb_ref, mb),
                (counts_ref, counts),
                (groups_ref, groups),
            )
        )
    ]
    for fetch in fetches(0)[:2] + small + fetches(0)[2:]:
        fetch.start()
    xh[...] = jnp.zeros(xh.shape, BF16)
    ogh[...] = jnp.zeros(ogh.shape, BF16)
    barrier = pltpu.get_barrier_semaphore()
    others(lambda r, p: pl.semaphore_signal(barrier, inc=1, device_id=(r, p), device_id_type=MESH))

    for fetch in small:
        fetch.wait()
    flip = lambda w: w.astype(F32).T.astype(BF16)
    taps = [cw[:, k, :] for k in range(4)]
    zero = jnp.zeros((ch, ch), BF16)
    for k in range(4):
        wc[:, k * ch : (k + 1) * ch] = taps[k] * 0.5
    for k in range(3):
        wd[:ch, k * ch : (k + 1) * ch] = dw[k] * 0.5
        wd[ch:, k * ch : (k + 1) * ch] = zero
        wdt[:, k * ch : (k + 1) * ch] = flip(dw[k]) * 0.5
    wm[...] = mw[...] * 0.5
    wd[:ch, 3 * ch :] = zero
    wd[ch:, 3 * ch :] = flip(mw[...]) * 0.5
    back = [flip(tap) for tap in taps]
    wct[:ch, :] = beside(back[3], back[1], zero)
    wct[ch:, :] = beside(zero, back[2], back[0])
    for k, line in enumerate((cb, db, mb)):
        biases[k] = jnp.broadcast_to(line[...] * 0.5, (EDGE, ch)).T

    lanes = span + 4 * EDGE
    frame = base - OFF + lax.broadcasted_iota(jnp.int32, (16, lanes), 1)
    for b in range(clips):
        valid = jnp.minimum(lax.shift_right_logical(counts[b], groups[b]), span * parts)
        mask = jnp.where((frame >= 0) & (frame < valid), 1.0, 0.0)
        mask_high[b] = mask[:8]
        mask_low[b] = mask.astype(BF16)

    for ref, at in ((gradm, OFF), (gradm, OFF + span), (grad, OFF + span)):
        ref[:, :, at : at + EDGE] = jnp.zeros((clips, ch, EDGE), BF16)
    for ref in (pconv, pdil, pmix, psum):
        ref[...] = jnp.zeros(ref.shape, F32)

    def masks(b, t, n):
        return mask_high[b, :, t + OFF : t + OFF + n]

    def low_masks(b, t, n):
        return mask_low[b, :, t + OFF : t + OFF + n]

    def put(ref, b, start, value):
        ref[b, :, start : start + value.shape[1]] = value

    has = (place > 0, place < parts - 1)
    other = (place - 1, place + 1)

    def moves(side):
        return [
            pltpu.make_async_remote_copy(
                src_ref=src.at[side],
                dst_ref=dst.at[1 - side],
                send_sem=send.at[side, k],
                recv_sem=recv.at[1 - side, k],
                device_id=(row, other[side]),
                device_id_type=MESH,
            )
            for k, (src, dst) in enumerate(((x_edge, xh), (og_edge, ogh)))
        ]

    near = EDGE // 2

    def swap(pair):
        return beside(pair[:, near:], pair[:, :near])

    def pack_edges():
        for side, at in ((0, OFF), (1, OFF + span - near)):
            for b in range(clips):
                x_edge[side, b] = beside(x0[b, :, at : at + near], x1[b, :, at : at + near])
            for b in range(0, clips, 2):
                og_edge[side, b // 2] = beside(bg[b, :, at : at + near], bg[b + 1, :, at : at + near])

    def spot(t, n):
        return slice(t + OFF, t + OFF + n)

    def gather(ref, where):
        return beside(*[ref[b, :, spot(t, n)] for b, t, n in where])

    def cuts(where):
        at = 0
        for b, t, n in where:
            yield b, t, n, slice(at, at + n)
            at += n

    def spread(refs, where, step, low):
        now, before, after = refs
        for b, t, n, cut in cuts(where):
            now[b, :, spot(t, n)] = low[:, cut]
            put(before, b, t + OFF + step, low[:, cut])
            put(after, b, t + OFF - step, low[:, cut])

    def lows(where):
        return beside(*[tall(low_masks(b, t, n), ch // 16) for b, t, n in where])

    def stage0(b, t, n):
        here = spot(t, n)
        low = lows([(b, t, n)])
        even = x0[b, :, here] * low
        x0[b, :, here] = even
        put(x0p, b, t + OFF - 1, even)
        put(x1m, b, t + OFF + 1, x1[b, :, here])

    def tiles(where):
        found = []
        for b, t, n, cut in cuts(where):
            at = t
            while at < t + n:
                stop = min([at + SUB, t + n] + [border for border in (0, span) if border > at])
                found.append(((b, at, stop - at), slice(cut.start + at - t, cut.start + stop - t)))
                at = stop
        return found

    def stage1(where):
        taps = stack(gather(x1m, where), gather(x0, where), gather(x1, where), gather(x0p, where))
        product = dot(wc[...], taps)
        yield
        for (b, t, n), cut in tiles(where):
            h = product[:, cut] + wide(biases[0], n // EDGE)
            value, s = gelu_parts(h)
            half[b, :, spot(t, n)] = h
            slope[b, :, spot(t, n)] = s
            spread((mid, midm, midp), [(b, t, n)], DILATION, value.astype(BF16) * lows([(b, t, n)]))
            yield

    def own(where):
        kept = [(b, max(t, 0), min(t + n, span) - max(t, 0)) for b, t, n in where]
        return kept, [
            slice(cut.start + kt - t, cut.start + kt - t + kn)
            for (b, t, n, cut), (_, kt, kn) in zip(cuts(where), kept)
        ]

    def inside_of(t, n):
        return 0 <= t and t + n <= span

    def stage2(where):
        taps = stack(gather(midm, where), gather(mid, where), gather(midp, where), gather(bg, where))
        both = dot(wd[...], taps)
        yield
        lows_of, kept = [], []
        for (b, t, n), cut in tiles(where):
            d = both[:ch, cut] + wide(biases[1], n // EDGE)
            value, s = gelu_parts(d)
            pg = both[ch:, cut] * s
            spread((pre, prem, prep), [(b, t, n)], DILATION, pg.astype(BF16))
            if inside_of(t, n):
                low = value.astype(BF16)
                gated[b, :, t : t + n] = low
                psum[1] += lane_groups(pg)
                lows_of.append(low)
                kept.append((b, t, n))
            yield
        low = beside(*lows_of)
        pmix[:, : ch + 16] += dot_t(gather(bg, kept), stack(low, jnp.ones((16, low.shape[1]), BF16)))
        yield

    def stage3(where, halo=None):
        mid_grad = dot(wdt[...], stack(gather(prep, where), gather(pre, where), gather(prem, where)))
        yield
        for (b, t, n), cut in tiles(where):
            mask = tall(masks(b, t, n), ch // 8)
            here = spot(t, n)
            g = (bg[b, :, here].astype(F32) + mid_grad[:, cut] * slope[b, :, here]) * mask
            low = g.astype(BF16)
            if inside_of(t, n):
                psum[0] += lane_groups(g)
                grad[b, :, spot(t, n)] = low
                put(gradm, b, t + OFF + 1, low)
            elif halo is not None:
                halo.append((b, t, low))
            yield

    def by_steps(sums, where):
        for b, t, n in where:
            for k in range(0, n, SUMS):
                sums([(b, t + k, min(SUMS, n - k))])
                yield

    def dilated_sums(where):
        pdil[...] += dot_t(
            stack(gather(pre, where), gather(prem, where)), stack(gather(mid, where), gather(midm, where))
        )

    def strided_sums(where):
        pconv[...] += dot_t(
            stack(gather(grad, where), gather(gradm, where)), stack(gather(x1m, where), gather(x0, where))
        )

    def pieces_of(b, margin):
        edges = [margin] + list(range(chunk, span - margin, chunk)) + [span - margin]
        return [(b, t, e - t) for t, e in zip(edges, edges[1:])]

    def first(b):
        for t in range(0, span, chunk):
            stage0(b, t, chunk)
            yield
        for piece in pieces_of(b, EDGE):
            yield from stage1([piece])

    def later(piece):
        b, t, n = piece
        skip = EDGE if t == 3 * EDGE else 0
        return b, t + skip, n - skip

    def second(b):
        for t in range(0, span, chunk):
            bg[b, :, spot(t, chunk)] = bg[b, :, spot(t, chunk)] * lows([(b, t, chunk)])
            yield
        for piece in pieces_of(b, 2 * EDGE):
            yield from stage2([piece])
        for piece in pieces_of(b, 3 * EDGE):
            yield from stage3([piece])
            yield from by_steps(dilated_sums, [piece])
            yield from by_steps(strided_sums, [later(piece)])

    def mix(main, side, ratio):
        done = object()
        while True:
            ended = [next(main, done) is done for _ in range(ratio)]
            if next(side, done) is done and ended[-1]:
                return

    def run(work):
        for _ in work:
            pass

    def edge(width):
        return [
            (b, -EDGE if side == 0 else span - width, width + EDGE) for b in range(clips) for side in range(2)
        ]

    def outside():
        for b, t, n in edge(0):
            side = 0 if t < 0 else 1
            low = lows([(b, t, n)])
            pair = xh[side, b]
            even = (swap(pair) if side == 0 else pair) * low
            odd = pair if side == 0 else swap(pair)
            x0[b, :, spot(t, n)] = even
            x1[b, :, spot(t, n)] = odd
            put(x0p, b, t + OFF - 1, even)
            put(x1m, b, t + OFF + 1, odd)
            pair = ogh[side, b // 2]
            bg[b, :, spot(t, n)] = (pair if side != b % 2 else swap(pair)) * low
        yield
        yield from stage1(edge(EDGE))
        yield from stage2(edge(2 * EDGE))
        yield from stage3(own(edge(3 * EDGE))[0])
        dilated_sums(own(edge(3 * EDGE))[0])
        strided_sums([(b, max(t, 0), 4 * EDGE) for b, t, _ in edge(3 * EDGE)])
        yield

    def arrive(b):
        for fetch in fetches(b):
            fetch.wait()

    for fetch in fetches(0)[:2]:
        fetch.wait()
    for fetch in fetches(1):
        fetch.start()
    run(first(0))
    fetches(0)[2].wait()
    arrive(1)
    for b in range(2, clips):
        for fetch in fetches(b):
            fetch.start()
    mix(second(0), first(1), RATIO)
    for b in range(2, clips):
        arrive(b)
    pack_edges()
    pl.semaphore_wait(barrier, count - 1)
    for side in range(2):
        @pl.when(has[side])
        def _():
            for move in moves(side):
                move.start()
    for b in range(1, clips - 1):
        mix(second(b), first(b + 1), RATIO)

    for side in range(2):
        @pl.when(has[side])
        def _():
            for move in moves(1 - side):
                move.wait_recv()
    mix(second(clips - 1), outside(), RATIO)

    flat = [pconv[...], pdil[:ch, :], beside(pdil[ch:, :ch], pmix[:, :ch])]
    lines = [jnp.sum(psum[k].T, axis=0, keepdims=True) for k in range(2)]
    lines.append(pmix[:, ch:].T[:1, :])
    lines = stack(*lines, jnp.zeros((ROWS - 3, ch), F32))
    flat.append(beside(lines, jnp.zeros_like(lines)))
    at = 0
    for block in flat:
        for start in range(0, block.shape[0], ROWS):
            parcel[at] = block[start : start + ROWS, :].astype(BF16)
            at += 1
    for home, start, n in owners:
        @pl.when(me != home)
        def _():
            pltpu.make_async_remote_copy(
                src_ref=parcel.at[pl.ds(start, n)],
                dst_ref=slots.at[lax.rem(me - home + count, count) - 1, pl.ds(0, n)],
                send_sem=send1,
                recv_sem=recv1,
                device_id=(home // parts, home % parts),
                device_id_type=MESH,
            ).start()

    halo = []
    run(stage3([(b, t, EDGE) for b in range(clips) for t in (-EDGE, span)], halo))
    for b, t, low in halo:
        if t < 0:
            put(gradm, b, t + OFF + 1, low)
        else:
            grad[b, :, spot(t, EDGE)] = low

    def third(b, carry):
        for t in range(0, span, chunk):
            here = slice(t + OFF, t + OFF + chunk)
            there = slice(t, t + chunk)
            low = low_masks(b, t, chunk)
            total = half[b, :, here] + dot(wm[...], gated[b, :, there]) + wide(biases[2], chunk // EDGE)
            outs[b, :, there] = total.astype(BF16) * tall(low + low, ch // 16)
            put(gradp, b, t + OFF - 1, grad[b, :, slice(t + OFF, t + OFF + chunk + EDGE)])
            dx = dot(wct[...], stack(gradm[b, :, here], grad[b, :, here], gradp[b, :, here]))
            dxs[b, :, there] = dx.astype(BF16) * tall(low, 2 * ch // 16)
        return carry

    lax.fori_loop(0, clips, third, 0)

    sizes = sorted({n for _, _, n in owners})
    blocks = parcel.shape[0]
    groups_of = [
        (n, [(home, start) for home, start, m in owners if m == n]) for n in sizes
    ]

    def is_one(homes):
        return functools.reduce(jnp.logical_or, [me == home for home, _ in homes])

    for n, homes in groups_of:
        @pl.when(is_one(homes))
        def _():
            start = sum(jnp.where(me == home, first_block, 0) for home, first_block in homes)
            mine = pl.ds(start, n)
            came = slots.at[:, pl.ds(0, n)]
            pltpu.make_async_copy(came, came, recv1).wait()
            total = parcel[mine].astype(F32)
            for k in range(count - 1):
                total = total + slots[k, :n].astype(F32)
            total_ref[mine] = total.astype(BF16)
            for k in range(1, count):
                target = lax.rem(me + k, count)
                pltpu.make_async_remote_copy(
                    src_ref=total_ref.at[mine],
                    dst_ref=total_ref.at[mine],
                    send_sem=send2,
                    recv_sem=recv2,
                    device_id=(target // parts, lax.rem(target, parts)),
                    device_id_type=MESH,
                ).start()

    for side in range(2):
        @pl.when(has[side])
        def _():
            for move in moves(side):
                move.wait_send()
    owner = is_one([(home, start) for home, start, _ in owners])
    for n, homes in groups_of:
        @pl.when(is_one(homes))
        def _():
            rest = total_ref.at[pl.ds(0, blocks - n)]
            pltpu.make_async_copy(rest, rest, recv2).wait()
            for _ in range(1, count):
                one = total_ref.at[pl.ds(0, n)]
                pltpu.make_async_copy(one, one, send2).wait()
            sent = parcel.at[pl.ds(0, blocks - n)]
            pltpu.make_async_copy(sent, sent, send1).wait()

    @pl.when(jnp.logical_not(owner))
    def _():
        pltpu.make_async_copy(total_ref, total_ref, recv2).wait()
        pltpu.make_async_copy(parcel, parcel, send1).wait()


def layer_call(rows, parts, clips, span, blocks):
    ch = 64
    lanes = span + 4 * EDGE
    vmem = pl.BlockSpec(memory_space=pltpu.VMEM)
    hbm = pl.BlockSpec(memory_space=pl.ANY)
    low = pltpu.VMEM((clips, ch, lanes), BF16)
    high = pltpu.VMEM((clips, ch, lanes), F32)
    dma = pltpu.SemaphoreType.DMA
    widest = max(n for _, _, n in owner_list(rows, parts, blocks))
    return pl.pallas_call(
        functools.partial(layer, rows, parts, owner_list(rows, parts, blocks)),
        name="layer",
        in_specs=[hbm] * 10,
        out_specs=[vmem, vmem, vmem],
        out_shape=[
            pltpu.VMEM((clips, ch, span), BF16),
            pltpu.VMEM((clips, 2 * ch, span), BF16),
            pltpu.VMEM((blocks, ROWS, 2 * ch), BF16),
        ],
        scratch_shapes=[
            pltpu.VMEM((ch, 4 * ch), BF16),
            pltpu.VMEM((2 * ch, 4 * ch), BF16),
            pltpu.VMEM((ch, ch), BF16),
            pltpu.VMEM((ch, 3 * ch), BF16),
            pltpu.VMEM((2 * ch, 3 * ch), BF16),
            pltpu.VMEM((3, ch, EDGE), F32),
        ]
        + [low] * 5
        + [high] * 2
        + [low] * 3
        + [pltpu.VMEM((clips, ch, span), BF16)]
        + [low] * 6
        + [
            pltpu.VMEM((2, clips, ch, EDGE), BF16),
            pltpu.VMEM((2, clips // 2, ch, EDGE), BF16),
            pltpu.VMEM((2, clips, ch, EDGE), BF16),
            pltpu.VMEM((2, clips // 2, ch, EDGE), BF16),
            pltpu.VMEM((2 * ch, 2 * ch), F32),
            pltpu.VMEM((2 * ch, 2 * ch), F32),
            pltpu.VMEM((ch, 2 * ch), F32),
            pltpu.VMEM((2, ch, EDGE), F32),
            pltpu.VMEM((clips, 8, lanes), F32),
            pltpu.VMEM((clips, 16, lanes), BF16),
            pltpu.VMEM((blocks, ROWS, 2 * ch), BF16),
            pltpu.VMEM((rows * parts - 1, widest, ROWS, 2 * ch), BF16),
            pltpu.SMEM((clips,), jnp.int32),
            pltpu.SMEM((clips,), jnp.int32),
            pltpu.VMEM((ch, 4, ch), BF16),
            pltpu.VMEM((3, ch, ch), BF16),
            pltpu.VMEM((ch, ch), BF16),
            pltpu.VMEM((1, ch), F32),
            pltpu.VMEM((1, ch), F32),
            pltpu.VMEM((1, ch), F32),
            dma((8,)),
            dma((clips, 3)),
            dma((2, 2)),
            dma((2, 2)),
            dma,
            dma,
            dma,
            dma,
        ],
        compiler_params=pltpu.CompilerParams(collective_id=0, has_side_effects=True, vmem_limit_bytes=54 << 20),
    )


def hand_over(out_in, clips_in, sums, *refs):
    out, clips = refs[:2]
    finals, (cg, cb, dg, db, mg, mb), (sem, small_sem) = refs[2:8], refs[8:14], refs[14:]
    ch = 64
    moves = []
    for b in range(out.shape[0]):
        for k, (src, dst) in enumerate(((out_in, out), (clips_in, clips))):
            moves.append(pltpu.make_async_copy(src.at[b], dst.at[b], sem.at[b, k]))
    for move in moves:
        move.start()
    at = lambda start, count: sums[start : start + count, :].astype(F32)
    low, high = at(0, ch), at(ch, ch)
    for k, block in enumerate((low[:, :ch], low[:, ch:], high[:, :ch], high[:, ch:])):
        cg[:, k, :] = block
    block = at(2 * ch, ch)
    dg[1] = block[:, :ch]
    dg[0] = block[:, ch:]
    block = at(3 * ch, ch)
    dg[2] = block[:, :ch]
    mg[...] = block[:, ch:]
    lines = at(4 * ch, 16)[:, :ch]
    for k, ref in enumerate((cb, db, mb)):
        ref[...] = lines[k : k + 1]
    for k, (src, dst) in enumerate(zip((cg, cb, dg, db, mg, mb), finals)):
        moves.append(pltpu.make_async_copy(src, dst, small_sem.at[k]))
        moves[-1].start()
    for move in moves:
        move.wait()


def hand_over_call(out, clips):
    ch = 64
    vmem = pl.BlockSpec(memory_space=pltpu.VMEM)
    hbm = pl.BlockSpec(memory_space=pl.ANY)
    shapes = [(ch, 4, ch), (1, ch), (3, ch, ch), (1, ch), (ch, ch), (1, ch)]
    like = lambda a: jax.ShapeDtypeStruct(a.shape, a.dtype)
    return pl.pallas_call(
        hand_over,
        name="hand_over",
        in_specs=[vmem] * 3,
        out_specs=[hbm] * 8,
        out_shape=[like(out), like(clips)] + [jax.ShapeDtypeStruct(s, F32) for s in shapes],
        scratch_shapes=[pltpu.VMEM(s, F32) for s in shapes]
        + [pltpu.SemaphoreType.DMA((out.shape[0], 2)), pltpu.SemaphoreType.DMA((6,))],
        compiler_params=pltpu.CompilerParams(vmem_limit_bytes=8 << 20),
    )


def body(rows, parts, clips_in, cw, cb, dw, db, mw, mb, counts, groups, out_grad):
    clips, ch, span = out_grad.shape
    blocks = (4 * ch + ROWS) // ROWS
    layer_out, clips_grad, sums = layer_call(rows, parts, clips, span, blocks)(
        counts, groups, clips_in, out_grad, cw.transpose(0, 2, 1), dw.transpose(2, 0, 1), mw, cb[None], db[None], mb[None]
    )
    layer_out, clips_grad, cg, cbg, dg, dbg, mg, mbg = hand_over_call(layer_out, clips_grad)(
        layer_out, clips_grad, sums.reshape(blocks * ROWS, 2 * ch)
    )
    return (layer_out, clips_grad, cg.transpose(0, 2, 1), cbg[0], dg.transpose(1, 2, 0), dbg[0], mg, mbg[0])


def solution(mesh):
    split = P("batch", None, "tm")
    placed = (split, P(), P(), P(), P(), P(), P(), P("batch"), P("batch"), split)
    return jax.shard_map(
        functools.partial(body, mesh.shape["batch"], mesh.shape["tm"]),
        mesh=mesh,
        in_specs=placed,
        out_specs=(split, split) + (P(),) * 6,
        check_vma=False,
    )
```
